512 devices in a mesh: slab: 128 (over z, y_hi, x), cross: 4 (over y_lo, core).
Axes of the slice: x: 4, y: 8 (y_hi: 4, y_lo: 2; y = y_hi * 2 + y_lo), z: 8, core: 2. Of those that a mesh axis runs over, the one named last changes fastest.
Arguments:
- features: bfloat16 [128, 4, 2, 96, 512], P('slab', 'cross'), may hold values from -6 to 6
- out_grad: bfloat16 [128, 4, 2, 192, 512], P('slab', 'cross'), may hold values from -6 to 6
- weights: bfloat16 [7, 96, 192], replicated, may hold values from -0.25 to 0.25
- conv_bias: float32 [192], replicated, may hold values from -1 to 1
- brick_count: int32 [128, 4], P('slab', 'cross'), may hold values from 2 to 2, as said below
- neighbours: int32 [128, 4, 2, 6], P('slab', 'cross'), may hold values from 3 to 20, as said below
- send_slab: int32 [128, 4, 2, 2], P('slab', 'cross'), may hold values from 0 to 12, as said below
- send_cross: int32 [128, 4, 2, 2], P('slab', 'cross'), may hold values from 2 to 12, as said below
Outputs:
- grad_features: bfloat16 [128, 4, 2, 96, 512], P('slab', 'cross')
- grad_weights: float32 [7, 96, 192], replicated
- grad_bias: float32 [192], replicated
The draws below stay inside these ranges and needn't reach their ends.
Inputs may be any that keep to these rules, and one draw needn't show every extreme that they name: Live bricks fill the first brick_count slots of a device; some device has all 2 slots live. `neighbours`: directions f = 0..5 are -x, +x, -y, +y, -z, +z. An entry below 12 names row 6 c + (f xor 1) of a live brick c of the same device; entries from 12 to 19 name received faces, the received slots of a list being named in list order; 20 is the zero row. No row other than the zero row is named twice; empty slots name only the zero row. `send_slab`: each row lists 6 b + f of live bricks in increasing order (f = 1 in row 0, f = 0 in row 1), then the value 6 * 2; in some device a row lists 2 faces. `send_cross`: each row lists 6 b + f of live bricks in increasing order (f = 3 in row 0, f = 2 in row 1), then the value 6 * 2; in some device a row lists 2 faces.
All inputs are finite; a program needn't handle non-finite values.
Results may differ from the reference program's by a relative error of at most 0.0075.
Values may be sent and summed in bfloat16 or wider, within the bound.
No kernel may reach another device: no remote copies, remote signals or barrier semaphores. Data moves between devices by JAX's collectives and lax.ppermute only.
A program may use at most 64 MiB of HBM per device.

```python
import math
from functools import partial
import jax
import jax.numpy as jnp
from jax import lax

CIN = 96
COUT = 192
EDGE = 8
BRICKS = 2
VOXELS = 512
ROWS_Z = 2
SLAB_FACES = 2
CROSS_FACES = 2
VOXEL_SLOTS = 524288
N_SLAB = 128
N_CROSS = 4


def shift_in(values, along, offset):
    length = values.shape[along]
    filler = jnp.zeros_like(lax.slice_in_dim(values, 0, 1, axis=along))
    if offset == 1:
        return jnp.concatenate([filler, lax.slice_in_dim(values, 0, length - 1, axis=along)], axis=along)
    return jnp.concatenate([lax.slice_in_dim(values, 1, length, axis=along), filler], axis=along)


def exclusive_count(flag_set):
    return (jnp.cumsum(flag_set, axis=-1) - flag_set).astype(jnp.int32)


def compact(flag_set, values, slot_count, filler):
    rank_of = exclusive_count(flag_set)
    placed = (flag_set[..., :, None] == 1) & (rank_of[..., :, None] == jnp.arange(slot_count, dtype=jnp.int32))
    filled = jnp.sum(jnp.where(placed, values[..., :, None], 0), axis=-2).astype(jnp.int32)
    used_slot = jnp.sum(placed.astype(jnp.int32), axis=-2).astype(jnp.int32)
    return (filled + (1 - used_slot) * filler).astype(jnp.int32)


def layout_draw(key):
    layout_key = jax.random.fold_in(key, 31)
    count_key = jax.random.fold_in(layout_key, 1)
    order_key = jax.random.fold_in(layout_key, 2)
    places = 2 * ROWS_Z
    wanted = jax.random.randint(count_key, (N_SLAB, N_CROSS, 1), BRICKS // 2 + 1, BRICKS + 1)
    scores = jax.random.randint(order_key, (N_SLAB, N_CROSS, places), 0, 1 << 20) * places + jnp.arange(places, dtype=jnp.int32)
    rank_of = jnp.argsort(jnp.argsort(scores, axis=-1), axis=-1)
    active = (rank_of < wanted).astype(jnp.int32)
    place_z = jnp.arange(places, dtype=jnp.int32) % ROWS_Z
    place_y = jnp.arange(places, dtype=jnp.int32) // ROWS_Z
    dropped = place_z >= ROWS_Z - 2
    first_set = 1 - ((place_y == 0) & dropped).astype(jnp.int32)
    second_set = 1 - ((place_y == 1) & dropped).astype(jnp.int32)
    active = active.at[0, 0].set(first_set).at[1, 0].set(first_set).at[0, 1].set(second_set)
    counts = jnp.sum(active, axis=-1).astype(jnp.int32)
    slot_of = exclusive_count(active)
    null_face = 6 * BRICKS
    zero_entry = 6 * BRICKS + 2 * SLAB_FACES + 2 * CROSS_FACES
    base_slab_low = 6 * BRICKS
    base_slab_high = base_slab_low + SLAB_FACES
    base_cross_low = base_slab_high + SLAB_FACES
    base_cross_high = base_cross_low + CROSS_FACES
    match_low = active * shift_in(active, 0, 1)
    match_high = active * shift_in(active, 0, -1)
    toward_low = jnp.where(match_low == 1, base_slab_low + exclusive_count(match_low), zero_entry)
    toward_high = jnp.where(match_high == 1, base_slab_high + exclusive_count(match_high), zero_entry)
    bottom_row = active[..., :ROWS_Z]
    top_row = active[..., ROWS_Z:]
    slot_bottom = slot_of[..., :ROWS_Z]
    slot_top = slot_of[..., ROWS_Z:]
    match_ylow = bottom_row * shift_in(top_row, 1, 1)
    match_yhigh = top_row * shift_in(bottom_row, 1, -1)
    minus_y = jnp.concatenate([jnp.where(match_ylow == 1, base_cross_low + exclusive_count(match_ylow), zero_entry), jnp.where(bottom_row == 1, slot_bottom * 6 + 3, zero_entry)], axis=-1)
    plus_y = jnp.concatenate([jnp.where(top_row == 1, slot_top * 6 + 2, zero_entry), jnp.where(match_yhigh == 1, base_cross_high + exclusive_count(match_yhigh), zero_entry)], axis=-1)
    prev_active = shift_in(active, 2, 1)
    prev_slot = shift_in(slot_of, 2, 1)
    next_active = shift_in(active, 2, -1)
    next_slot = shift_in(slot_of, 2, -1)
    minus_z = jnp.where((place_z > 0) & (prev_active == 1), prev_slot * 6 + 5, zero_entry)
    plus_z = jnp.where((place_z < ROWS_Z - 1) & (next_active == 1), next_slot * 6 + 4, zero_entry)
    by_place = jnp.stack([toward_low, toward_high, minus_y, plus_y, minus_z, plus_z], axis=-1)
    chosen = (active[..., :, None] == 1) & (slot_of[..., :, None] == jnp.arange(BRICKS, dtype=jnp.int32))
    link_rows = jnp.sum(jnp.where(chosen[..., None], by_place[..., :, None, :], 0), axis=2)
    used_slot = jnp.sum(chosen.astype(jnp.int32), axis=2)[..., None]
    link_rows = (link_rows + (1 - used_slot) * zero_entry).astype(jnp.int32)
    slab_lists = jnp.stack([compact(match_high, slot_of * 6 + 1, SLAB_FACES, null_face), compact(match_low, slot_of * 6, SLAB_FACES, null_face)], axis=2)
    cross_lists = jnp.stack([compact(match_yhigh, slot_top * 6 + 3, CROSS_FACES, null_face), compact(match_ylow, slot_bottom * 6 + 2, CROSS_FACES, null_face)], axis=2)
    return (counts, link_rows, slab_lists, cross_lists)


def draw_brick_count(key, part):
    return layout_draw(key)[0]


def draw_neighbours(key, part):
    return layout_draw(key)[1]


def draw_send_slab(key, part):
    return layout_draw(key)[2]


def draw_send_cross(key, part):
    return layout_draw(key)[3]


def level_of(stream_key, dims, shards, low, largest):
    gain = 1.0
    for position, parts in shards:
        heights = jax.random.uniform(jax.random.fold_in(jax.random.fold_in(stream_key, 6), position), (parts,), jnp.float32, low / len(shards), largest / len(shards))
        gain = gain * jnp.repeat(jnp.exp(heights), dims[position] // parts).reshape((-1,) + (1,) * (len(dims) - 1 - position))
    return gain


def bell_draw(rng, shape, scale, limit, cuts=(), held_as=jnp.bfloat16):
    drawn = jax.random.normal(rng, shape, jnp.float32) * scale
    if len(cuts) > 0:
        drawn = level_of(rng, shape, cuts, -0.22, 0.18) * drawn
    return jnp.clip(drawn, min=-limit, max=limit).astype(held_as)


def setup_inputs(seed: int = 0) -> dict:
    splits = jax.random.split(jax.random.key(seed), 9)
    features = bell_draw(splits[0], (N_SLAB, N_CROSS, BRICKS, CIN, VOXELS), 1.0, 6.0, ((0, 128), (1, 4)))
    out_grad = bell_draw(splits[1], (N_SLAB, N_CROSS, BRICKS, COUT, VOXELS), 1.0, 6.0, ((0, 128), (1, 4)))
    weights = bell_draw(splits[2], (7, CIN, COUT), (7 * CIN) ** -0.5, 0.25)
    conv_bias = jnp.clip(jax.random.uniform(splits[3], (COUT,), jnp.float32, -1.0, 1.0), -1.0, 1.0)
    brick_count = draw_brick_count(jax.random.fold_in(splits[8], 71), 0)
    neighbours = draw_neighbours(jax.random.fold_in(splits[8], 71), 0)
    send_slab = draw_send_slab(jax.random.fold_in(splits[8], 71), 0)
    send_cross = draw_send_cross(jax.random.fold_in(splits[8], 71), 0)
    return dict(features=features, out_grad=out_grad, weights=weights, conv_bias=conv_bias, brick_count=brick_count, neighbours=neighbours, send_slab=send_slab, send_cross=send_cross)


highest = lax.Precision.HIGHEST

def face_layers(bricks):
    number, channels = (bricks.shape[0], bricks.shape[1])
    boundary = [bricks[:, :, 0], bricks[:, :, -1], bricks[:, :, :, 0], bricks[:, :, :, -1], bricks[:, :, :, :, 0], bricks[:, :, :, :, -1]]
    return jnp.stack([layer_face.reshape(number, channels, -1) for layer_face in boundary], axis=1)

def tap_field(tap_index, bricks, beside):
    if tap_index == 0:
        return bricks
    if tap_index == 1:
        return jnp.concatenate([beside[:, 0][:, :, None], bricks[:, :, :-1]], axis=2)
    if tap_index == 2:
        return jnp.concatenate([bricks[:, :, 1:], beside[:, 1][:, :, None]], axis=2)
    if tap_index == 3:
        return jnp.concatenate([beside[:, 2][:, :, :, None], bricks[:, :, :, :-1]], axis=3)
    if tap_index == 4:
        return jnp.concatenate([bricks[:, :, :, 1:], beside[:, 3][:, :, :, None]], axis=3)
    if tap_index == 5:
        return jnp.concatenate([beside[:, 4][..., None], bricks[..., :-1]], axis=4)
    return jnp.concatenate([bricks[..., 1:], beside[:, 5][..., None]], axis=4)

def spread_rows(values, indices, total_rows):
    selector = (indices[:, None] == jnp.arange(total_rows, dtype=jnp.int32)[None, :]).astype(jnp.float32)
    return jnp.einsum('mk,md->kd', selector, values, precision=highest)

def silu_slope(pre_act):
    sigmoid_pre = jax.nn.sigmoid(pre_act)
    return sigmoid_pre * (1.0 + pre_act * (1.0 - sigmoid_pre))

def shift_axis(values, along, offset):
    length = values.shape[along]
    filler = jnp.zeros_like(lax.slice_in_dim(values, 0, 1, axis=along))
    if offset == 1:
        return jnp.concatenate([filler, lax.slice_in_dim(values, 0, length - 1, axis=along)], axis=along)
    return jnp.concatenate([lax.slice_in_dim(values, 1, length, axis=along), filler], axis=along)

def face_adjoint(values):
    number, channels = (values.shape[0], values.shape[2])
    edge_len = EDGE
    zero_cube = jnp.zeros((number, channels, edge_len, edge_len, edge_len), jnp.float32)
    _, face_pull = jax.vjp(face_layers, zero_cube)
    return face_pull(values)[0].reshape(number, channels, -1)

def device_terms(cubes, face_table, link_rows, live_count, upstream, weights, conv_bias):
    number, channels, edge_len = (cubes.shape[0], cubes.shape[1], cubes.shape[2])
    beside = jnp.take(face_table, link_rows, axis=0).reshape(number, 6, channels, edge_len, edge_len)
    fields = [tap_field(tap_index, cubes, beside).reshape(number, channels, -1) for tap_index in range(7)]
    pre_act = conv_bias[None, :, None]
    for tap_index in range(7):
        pre_act = pre_act + jnp.einsum('io,biv->bov', weights[tap_index].astype(jnp.float32), fields[tap_index].astype(jnp.float32), precision=highest)
    live_slot = jnp.arange(number, dtype=jnp.int32) < live_count
    grad_pre = jnp.where(live_slot[:, None, None], upstream.astype(jnp.float32) * silu_slope(pre_act), 0.0).astype(jnp.bfloat16)
    grad_wide = grad_pre.astype(jnp.float32)
    weight_terms = jnp.stack([jnp.einsum('biv,bov->io', fields[tap_index].astype(jnp.float32), grad_wide, precision=highest) for tap_index in range(7)])
    bias_terms = lax.optimization_barrier(jnp.sum(grad_wide, axis=(0, 2)))
    zero_cube = jnp.zeros(cubes.shape, jnp.float32)
    zero_beside = jnp.zeros(beside.shape, jnp.float32)
    grad_cube = zero_cube
    grad_beside = zero_beside
    for tap_index in range(7):
        tap_grad = jnp.einsum('io,bov->biv', weights[tap_index].astype(jnp.float32), grad_wide, precision=highest).reshape(cubes.shape)
        _, pullback = jax.vjp(partial(tap_field, tap_index), zero_cube, zero_beside)
        part_cube, part_beside = pullback(tap_grad)
        grad_cube = grad_cube + part_cube
        grad_beside = grad_beside + part_beside
    grad_table = spread_rows(grad_beside.reshape(number * 6, -1), link_rows, face_table.shape[0])
    return (grad_cube.reshape(number, channels, -1), grad_table, weight_terms, bias_terms)

def reference(features, out_grad, weights, conv_bias, brick_count, neighbours, send_slab, send_cross):
    n_slab, n_cross, number, channels, voxels = features.shape
    out_channels = out_grad.shape[3]
    edge_len = EDGE
    row_width = channels * edge_len * edge_len
    local_rows = number * 6
    slab_faces = send_slab.shape[3]
    cross_faces = send_cross.shape[3]
    cubes = features.reshape(n_slab, n_cross, number, channels, edge_len, edge_len, edge_len)
    own_faces = jax.vmap(jax.vmap(face_layers))(cubes).reshape(n_slab, n_cross, local_rows, row_width)
    zero_row = jnp.zeros((n_slab, n_cross, 1, row_width), features.dtype)
    padded = jnp.concatenate([own_faces, zero_row], axis=2)
    pick_rows = jax.vmap(jax.vmap(partial(jnp.take, axis=0)))
    slab_sent = pick_rows(padded, send_slab)
    cross_sent = pick_rows(padded, send_cross)
    slab_low = shift_axis(slab_sent[:, :, 0], 0, 1)
    slab_high = shift_axis(slab_sent[:, :, 1], 0, -1)
    cross_low = shift_axis(cross_sent[:, :, 0], 1, 1)
    cross_high = shift_axis(cross_sent[:, :, 1], 1, -1)
    face_table = jnp.concatenate([own_faces, slab_low, slab_high, cross_low, cross_high, zero_row], axis=2)
    table_rows = face_table.shape[2]
    devices = n_slab * n_cross

    def one_device(inputs):
        return device_terms(inputs[0], inputs[1], inputs[2], inputs[3], inputs[4], weights, conv_bias)
    grad_cube, grad_table, weight_terms, bias_terms = lax.map(one_device, (cubes.reshape(devices, number, channels, edge_len, edge_len, edge_len), face_table.reshape(devices, table_rows, row_width), neighbours.reshape(devices, local_rows), brick_count.reshape(devices), out_grad.reshape(devices, number, out_channels, voxels)))
    norm_scale = 1.0 / math.sqrt(VOXEL_SLOTS)
    grad_weights = lax.optimization_barrier(jnp.sum(weight_terms, axis=0)) * norm_scale
    grad_bias = lax.optimization_barrier(jnp.sum(bias_terms, axis=0)) * norm_scale
    grad_table = grad_table.reshape(n_slab, n_cross, table_rows, row_width)
    first_low = local_rows
    first_high = first_low + slab_faces
    first_cross_low = first_high + slab_faces
    first_cross_high = first_cross_low + cross_faces
    back_slab = jnp.stack([shift_axis(grad_table[:, :, first_low:first_high], 0, -1), shift_axis(grad_table[:, :, first_high:first_cross_low], 0, 1)], axis=2)
    back_cross = jnp.stack([shift_axis(grad_table[:, :, first_cross_low:first_cross_high], 1, -1), shift_axis(grad_table[:, :, first_cross_high:first_cross_high + cross_faces], 1, 1)], axis=2)
    spread_all = jax.vmap(jax.vmap(partial(spread_rows, total_rows=local_rows + 1)))
    face_grad = grad_table[:, :, :local_rows]
    face_grad = face_grad + spread_all(back_slab.reshape(n_slab, n_cross, 2 * slab_faces, row_width), send_slab.reshape(n_slab, n_cross, 2 * slab_faces))[:, :, :local_rows]
    face_grad = face_grad + spread_all(back_cross.reshape(n_slab, n_cross, 2 * cross_faces, row_width), send_cross.reshape(n_slab, n_cross, 2 * cross_faces))[:, :, :local_rows]
    face_back = jax.vmap(jax.vmap(face_adjoint))(face_grad.reshape(n_slab, n_cross, number, 6, channels, edge_len * edge_len))
    grad_total = grad_cube.reshape(n_slab, n_cross, number, channels, voxels) + face_back
    return (grad_total.astype(jnp.bfloat16), grad_weights, grad_bias)
```

```python
import math

import jax
import jax.numpy as jnp
from jax import lax
from jax.experimental import pallas as pl
from jax.experimental.pallas import tpu as pltpu
from jax.sharding import PartitionSpec as P

EDGE = 8
LAYER = EDGE * EDGE
TILE = 2 * LAYER
PACK = 16
f32 = jnp.float32
bf16 = jnp.bfloat16
VMEM = pl.BlockSpec(memory_space=pltpu.VMEM)
SMEM = pl.BlockSpec(memory_space=pltpu.SMEM)


def nn(a, b):
    return lax.dot_general(a, b, (((1,), (0,)), ((), ())), preferred_element_type=f32)


def nt(a, b):
    return lax.dot_general(a, b, (((1,), (1,)), ((), ())), preferred_element_type=f32)


def tn(a, b):
    return lax.dot_general(a, b, (((0,), (0,)), ((), ())), preferred_element_type=f32)


def layer_map(axis, voxels):
    row = lax.broadcasted_iota(jnp.int32, (TILE, voxels), 0)
    v = lax.broadcasted_iota(jnp.int32, (TILE, voxels), 1)
    x, y, z = v >> 6, (v >> 3) & 7, v & 7
    along, beside = (y, x * EDGE + z) if axis == 1 else (z, x * EDGE + y)
    low = (along == 0) & (row == beside)
    high = (along == EDGE - 1) & (row == beside + LAYER)
    return jnp.where(low | high, 1.0, 0.0).astype(bf16)


def low_half(rows):
    return lax.broadcasted_iota(jnp.int32, (rows, TILE), 1) < LAYER


def x_faces(brick):
    return jnp.where(low_half(brick.shape[0]), brick[:, :TILE], brick[:, -TILE:])


def doubled(tile):
    turned = pltpu.roll(tile, LAYER, 1)
    half = low_half(tile.shape[0])
    return jnp.where(half, tile, turned), jnp.where(half, turned, tile)


def send_kernel(features, slab_list, cross_list, *sends):
    number, channels, voxels = features.shape[2:]
    y_map = layer_map(1, voxels)
    half = low_half(channels)
    tables = ([], [])
    for b in range(number):
        brick = features[0, 0, b]
        tables[0].append(doubled(x_faces(brick.astype(f32))))
        tables[1].append(doubled(nt(brick, y_map)))
    for axis, listed in enumerate((slab_list, cross_list)):
        for row in range(2):
            side = 1 - row
            picked = []
            for k in range(2):
                entry = listed[0, 0, row, k]
                value = jnp.zeros((channels, TILE), f32)
                for b in range(number):
                    value = jnp.where(entry == 6 * b + 2 * axis + side, tables[axis][b][side], value)
                picked.append(value)
            sends[2 * axis + row][...] = jnp.where(half, picked[0], picked[1]).astype(bf16)


def main_kernel(features, upstream, weights, bias, count, links, slab_low, slab_high, cross_low, cross_high,
                back_slab_low, back_slab_high, back_cross_low, back_cross_high, terms, partial,
                fields, taps, table, grad, marks, table_grad):
    number, channels, voxels = features.shape[2:]
    out_channels = upstream.shape[3]
    depth = 7 * channels
    total = number * voxels
    own = 6 * number
    half = low_half(channels)
    lane = lax.broadcasted_iota(jnp.int32, (channels, total), 1)
    v = lane & (voxels - 1)
    coords = (v >> 6, (v >> 3) & 7, v & 7)
    strides = (LAYER, EDGE, 1)
    for axis in (1, 2):
        marks[TILE * (axis - 1):TILE * axis] = layer_map(axis, voxels)

    cubes = jnp.concatenate([features[0, 0, b] for b in range(number)], axis=1)
    cubes32 = cubes.astype(f32)
    for b in range(number):
        brick = features[0, 0, b]
        table[6 * b], table[6 * b + 1] = doubled(x_faces(brick.astype(f32)))
        sides = nt(brick, marks[...])
        table[6 * b + 2], table[6 * b + 3] = doubled(sides[:, :TILE])
        table[6 * b + 4], table[6 * b + 5] = doubled(sides[:, TILE:])
    for k, received in enumerate((slab_low, slab_high, cross_low, cross_high)):
        table[own + 2 * k], table[own + 2 * k + 1] = doubled(received[...].astype(f32))
    table[own + 8] = jnp.zeros((channels, TILE), f32)

    fields[:channels] = cubes
    for axis in range(3):
        expanded = []
        for b in range(number):
            tile = jnp.where(half, table[links[0, 0, b, 2 * axis]], table[links[0, 0, b, 2 * axis + 1]])
            if axis == 0:
                gap = jnp.zeros((channels, voxels - 2 * TILE), f32)
                expanded.append(jnp.concatenate([tile, gap, tile], axis=1))
            else:
                expanded.append(nn(tile.astype(bf16), marks[TILE * (axis - 1):TILE * axis]))
        outer = jnp.concatenate(expanded, axis=1)
        low = jnp.where(coords[axis] == 0, outer, pltpu.roll(cubes32, strides[axis], 1))
        high = jnp.where(coords[axis] == EDGE - 1, outer, pltpu.roll(cubes32, total - strides[axis], 1))
        fields[channels * (2 * axis + 1):channels * (2 * axis + 2)] = low.astype(bf16)
        fields[channels * (2 * axis + 2):channels * (2 * axis + 3)] = high.astype(bf16)
    fields[depth:] = jnp.ones((PACK, total), bf16)

    first = bias[...].astype(bf16)
    rest = bias[...] - first.astype(f32)
    second = rest.astype(bf16)
    third = (rest - second.astype(f32)).astype(bf16)
    row = lax.broadcasted_iota(jnp.int32, (PACK, out_channels), 0)
    extra = jnp.where(row == 0, first.astype(f32),
                      jnp.where(row == 1, second.astype(f32), jnp.where(row == 2, third.astype(f32), 0.0)))
    taps[:depth] = weights[...]
    taps[depth:] = extra.astype(bf16)

    pre = tn(taps[...], fields[...])
    grad[out_channels:] = jnp.zeros((grad.shape[0] - out_channels, total), bf16)
    for b in range(number):
        part = pre[:, voxels * b:voxels * (b + 1)]
        s = jax.nn.sigmoid(part)
        value = upstream[0, 0, b].astype(f32) * (s * (1.0 + part * (1.0 - s)))
        grad[:out_channels, voxels * b:voxels * (b + 1)] = jnp.where(b < count[0, 0], value, 0.0).astype(bf16)

    found = nt(fields[...], grad[...])
    middle = depth // 2
    terms[:depth] = found[:depth, :TILE].astype(bf16)
    terms[depth:depth + middle] = (found[:middle, TILE:] + pltpu.roll(found[middle:depth, TILE:], LAYER, 1)).astype(bf16)
    row = lax.broadcasted_iota(jnp.int32, (PACK, TILE), 0)
    terms[depth + middle:] = jnp.where(row == 0, found[depth:, :TILE],
                                       jnp.where(row == 1, found[depth:, TILE:], 0.0)).astype(bf16)

    table_grad[...] = jnp.zeros(table_grad.shape, f32)
    live = grad[:out_channels]
    summed = nn(weights[:channels], live)
    for axis in range(3):
        low = nn(weights[channels * (2 * axis + 1):channels * (2 * axis + 2)], live)
        high = nn(weights[channels * (2 * axis + 2):channels * (2 * axis + 3)], live)
        at = coords[axis]
        summed = summed + jnp.where(at < EDGE - 1, pltpu.roll(low, total - strides[axis], 1), 0.0)
        summed = summed + jnp.where(at > 0, pltpu.roll(high, strides[axis], 1), 0.0)
        edge = jnp.where(at == 0, low, high)
        for b in range(number):
            brick = edge[:, voxels * b:voxels * (b + 1)]
            if axis == 0:
                tile = x_faces(brick)
            else:
                tile = nt(brick.astype(bf16), marks[TILE * (axis - 1):TILE * axis])
            to_low, to_high = doubled(tile)
            table_grad[links[0, 0, b, 2 * axis]] = to_low
            table_grad[links[0, 0, b, 2 * axis + 1]] = to_high
    for k, back in enumerate((back_slab_low, back_slab_high, back_cross_low, back_cross_high)):
        back[...] = jnp.where(half, table_grad[own + 2 * k], table_grad[own + 2 * k + 1]).astype(bf16)
    for b in range(number):
        parts = summed[:, voxels * b:voxels * (b + 1)]
        for axis in range(3):
            tile = jnp.where(half, table_grad[6 * b + 2 * axis], table_grad[6 * b + 2 * axis + 1])
            parts = parts + spread(tile, axis, marks, voxels)
        partial[:, voxels * b:voxels * (b + 1)] = parts


def spread(tile, axis, marks, voxels):
    if axis > 0:
        return nn(tile.astype(bf16), marks[TILE * (axis - 1):TILE * axis])
    half = low_half(tile.shape[0])
    gap = jnp.zeros((tile.shape[0], voxels - 2 * TILE), f32)
    return jnp.concatenate([jnp.where(half, tile, 0.0), gap, jnp.where(half, 0.0, tile)], axis=1)


def sum_kernel(owners, partial, slab_list, cross_list, slab_first, slab_second, cross_first, cross_second,
               arrived, shared, result, marks):
    rows = arrived.shape[0]
    chunk = rows // owners
    step = max(chunk, PACK)
    value = jnp.sum(arrived[...].astype(f32).reshape(rows // step, step, TILE), axis=0)
    turn = chunk
    while turn < step:
        value = value + pltpu.roll(value, turn, 0)
        turn *= 2
    shared[...] = jnp.broadcast_to(value.astype(bf16)[None], (rows // step, step, TILE)).reshape(rows, TILE)

    number, channels, voxels = result.shape[2:]
    half = low_half(channels)
    marks[...] = layer_map(1, voxels)
    groups = ((slab_list, (slab_first, slab_second)), (cross_list, (cross_first, cross_second)))
    faces = [[doubled(back[...].astype(f32)) for back in backs] for _, backs in groups]
    for b in range(number):
        parts = partial[:, voxels * b:voxels * (b + 1)]
        for axis, (listed, _) in enumerate(groups):
            sides = []
            for side in range(2):
                value = jnp.zeros((channels, TILE), f32)
                for k in range(2):
                    entry = listed[0, 0, 1 - side, k]
                    value = value + jnp.where(entry == 6 * b + 2 * axis + side, faces[axis][1 - side][k], 0.0)
                sides.append(value)
            parts = parts + spread(jnp.where(half, sides[0], sides[1]), axis, marks, voxels)
        result[0, 0, b] = parts.astype(bf16)


def unpack_kernel(scale, gathered, kernel_grad, bias_grad):
    taps, channels, out_channels = kernel_grad.shape
    depth = taps * channels
    middle = depth // 2
    wide = gathered[...].astype(f32) * scale
    rest = wide[depth:depth + middle]
    second = jnp.concatenate([rest, pltpu.roll(rest, LAYER, 1)], axis=0)
    for tap in range(taps):
        rows = slice(channels * tap, channels * (tap + 1))
        kernel_grad[tap, :, :TILE] = wide[rows]
        kernel_grad[tap, :, TILE:] = second[rows, :out_channels - TILE]
    bias_grad[:, :TILE] = wide[depth + middle:depth + middle + 1]
    bias_grad[:, TILE:] = wide[depth + middle + 1:depth + middle + 2, :out_channels - TILE]


def shifted(value, axis, steps):
    count = lax.axis_size(axis)
    initial, last = (max(0, -steps), min(count, count - steps))
    return lax.ppermute(value, axis, [(source, source + steps) for source in range(initial, last)])


def shape(dims, dtype):
    return jax.ShapeDtypeStruct(dims, dtype)


def local(features, out_grad, weights, conv_bias, brick_count, neighbours, send_slab, send_cross):
    number, channels, voxels = features.shape[2:]
    out_channels = out_grad.shape[3]
    depth = 7 * channels
    total = number * voxels
    owners = lax.axis_size("slab") * lax.axis_size("cross")
    face_pair = shape((channels, TILE), bf16)
    limit = pltpu.CompilerParams(vmem_limit_bytes=48 * 2**20)

    sends = pl.pallas_call(
        send_kernel,
        out_shape=[face_pair] * 4,
        in_specs=[VMEM, SMEM, SMEM],
        out_specs=[VMEM] * 4,
        compiler_params=limit,
    )(features, send_slab, send_cross)
    slab_low = shifted(sends[0], "slab", 1)
    slab_high = shifted(sends[1], "slab", -1)
    cross_low = shifted(sends[2], "cross", 1)
    cross_high = shifted(sends[3], "cross", -1)

    packed = shape((depth * 3 // 2 + PACK, TILE), bf16)
    *backs, terms, partial = pl.pallas_call(
        main_kernel,
        out_shape=[face_pair] * 4 + [packed, shape((channels, total), f32)],
        in_specs=[VMEM] * 4 + [SMEM, SMEM] + [VMEM] * 4,
        out_specs=[VMEM] * 6,
        scratch_shapes=[
            pltpu.VMEM((depth + PACK, total), bf16),
            pltpu.VMEM((depth + PACK, out_channels), bf16),
            pltpu.VMEM((6 * number + 9, channels, TILE), f32),
            pltpu.VMEM((2 * TILE, total), bf16),
            pltpu.VMEM((2 * TILE, voxels), bf16),
            pltpu.VMEM((6 * number + 9, channels, TILE), f32),
        ],
        compiler_params=limit,
    )(features, out_grad, weights.reshape(depth, out_channels), conv_bias.reshape(1, out_channels), brick_count,
      neighbours, slab_low, slab_high, cross_low, cross_high)
    slab_first = shifted(backs[0], "slab", -1)
    slab_second = shifted(backs[1], "slab", 1)
    cross_first = shifted(backs[2], "cross", -1)
    cross_second = shifted(backs[3], "cross", 1)

    arrived = lax.all_to_all(terms, ("slab", "cross"), 0, 0, tiled=True)
    shared, grad_features = pl.pallas_call(
        lambda *refs: sum_kernel(owners, *refs),
        out_shape=[packed, shape(features.shape, bf16)],
        in_specs=[VMEM, SMEM, SMEM] + [VMEM] * 5,
        out_specs=[VMEM] * 2,
        scratch_shapes=[pltpu.VMEM((TILE, voxels), bf16)],
        compiler_params=limit,
    )(partial, send_slab, send_cross, slab_first, slab_second, cross_first, cross_second, arrived)
    gathered = lax.all_to_all(shared, ("slab", "cross"), 0, 0, tiled=True)
    scale = 1.0 / math.sqrt(owners * total)
    kernel_grad, bias_grad = pl.pallas_call(
        lambda *refs: unpack_kernel(scale, *refs),
        out_shape=[shape(weights.shape, f32), shape((1, out_channels), f32)],
        in_specs=[VMEM],
        out_specs=[VMEM] * 2,
        compiler_params=limit,
    )(gathered)
    return grad_features, kernel_grad, bias_grad.reshape(out_channels)


def solution(mesh):
    in_specs = (
        P("slab", "cross", None, None, None),
        P("slab", "cross", None, None, None),
        P(),
        P(),
        P("slab", "cross"),
        P("slab", "cross", None, None),
        P("slab", "cross", None, None),
        P("slab", "cross", None, None),
    )
    out_specs = (P("slab", "cross", None, None, None), P(), P())
    return jax.shard_map(local, mesh=mesh, in_specs=in_specs, out_specs=out_specs, check_vma=False)
```

```python
import math

import jax
import jax.numpy as jnp
from jax import lax
from jax.experimental import pallas as pl
from jax.experimental.pallas import tpu as pltpu
from jax.sharding import PartitionSpec as P

EDGE = 8
LAYER = EDGE * EDGE
TILE = 2 * LAYER
PACK = 16
FIRST = 60 * 2**20
MIDDLE = 56_000_000
NEAR = (0, 1, 2, 3, 6)
f32 = jnp.float32
bf16 = jnp.bfloat16
VMEM = pl.BlockSpec(memory_space=pltpu.VMEM)
SMEM = pl.BlockSpec(memory_space=pltpu.SMEM)
HBM = pl.BlockSpec(memory_space=pltpu.HBM)


def nn(a, b):
    return lax.dot_general(a, b, (((1,), (0,)), ((), ())), preferred_element_type=f32)


def nt(a, b):
    return lax.dot_general(a, b, (((1,), (1,)), ((), ())), preferred_element_type=f32)


def tn(a, b):
    return lax.dot_general(a, b, (((0,), (0,)), ((), ())), preferred_element_type=f32)


def layer_map(axis, voxels):
    row = lax.broadcasted_iota(jnp.int32, (TILE, voxels), 0)
    v = lax.broadcasted_iota(jnp.int32, (TILE, voxels), 1)
    x, y, z = v >> 6, (v >> 3) & 7, v & 7
    along, beside = (y, x * EDGE + z) if axis == 1 else (z, x * EDGE + y)
    low = (along == 0) & (row == beside)
    high = (along == EDGE - 1) & (row == beside + LAYER)
    return jnp.where(low | high, 1.0, 0.0).astype(bf16)


def low_half(rows):
    return lax.broadcasted_iota(jnp.int32, (rows, TILE), 1) < LAYER


def x_faces(brick):
    return jnp.where(low_half(brick.shape[0]), brick[:, :TILE], brick[:, -TILE:])


def doubled(tile):
    turned = pltpu.roll(tile, LAYER, 1)
    half = low_half(tile.shape[0])
    return jnp.where(half, tile, turned), jnp.where(half, turned, tile)


def fetch(sources, targets, arrivals):
    copies = [pltpu.make_async_copy(a, b, arrivals.at[k]) for k, (a, b) in enumerate(zip(sources, targets))]
    for copy in copies:
        copy.start()
    return copies


def choose(axis, even, odd):
    return jnp.where((lax.axis_index(axis) & 1) == 0, even, odd)


def to_peers(refs, up, down, cross_up, cross_down):
    for ref, tile in zip(refs, (choose("slab", down, up), choose("slab", up, down),
                                choose("cross", cross_down, cross_up), choose("cross", cross_up, cross_down))):
        ref[...] = tile.astype(bf16)


def from_peers(refs):
    far, near, cross_far, cross_near = [ref[...].astype(f32) for ref in refs]
    return (choose("slab", far, near), choose("slab", near, far),
            choose("cross", cross_far, cross_near), choose("cross", cross_near, cross_far))


def send_kernel(features_in, slab_in, cross_in, *refs):
    faces, (features, slab_list, cross_list, arrivals) = refs[:4], refs[4:]
    copies = fetch((features_in, slab_in, cross_in), (features, slab_list, cross_list), arrivals)
    number, channels, voxels = features.shape[2:]
    y_map = layer_map(1, voxels)
    for copy in copies:
        copy.wait()
    half = low_half(channels)
    tables = ([], [])
    for b in range(number):
        brick = features[0, 0, b]
        tables[0].append(doubled(x_faces(brick.astype(f32))))
        tables[1].append(doubled(nt(brick, y_map)))
    sends = []
    for axis, listed in enumerate((slab_list, cross_list)):
        for row in range(2):
            side = 1 - row
            picked = []
            for k in range(2):
                entry = listed[0, 0, row, k]
                value = jnp.zeros((channels, TILE), f32)
                for b in range(number):
                    value = jnp.where(entry == 6 * b + 2 * axis + side, tables[axis][b][side], value)
                picked.append(value)
            sends.append(jnp.where(half, picked[0], picked[1]))
    to_peers(faces, *sends)


def main_kernel(features_in, weights_in, upstream_in, bias_in, count_in, links_in, *refs):
    received, sent, (terms, partial), refs = refs[:4], refs[4:8], refs[8:10], refs[10:]
    features, weights, upstream, bias, count, links, fields, grad, taps, table, marks, table_grad, arrivals = refs
    copies = fetch(
        (features_in, links_in, weights_in, bias_in, count_in, upstream_in),
        (features, links, weights, bias, count, upstream), arrivals)
    number, channels, voxels = features.shape[2:]
    out_channels = upstream.shape[3]
    depth = 7 * channels
    total = number * voxels
    own = 6 * number
    half = low_half(channels)
    lane = lax.broadcasted_iota(jnp.int32, (channels, total), 1)
    v = lane & (voxels - 1)
    coords = (v >> 6, (v >> 3) & 7, v & 7)
    strides = (LAYER, EDGE, 1)
    for axis in (1, 2):
        marks[TILE * (axis - 1):TILE * axis] = layer_map(axis, voxels)
    copies[0].wait()

    cubes = jnp.concatenate([features[0, 0, b] for b in range(number)], axis=1)
    cubes32 = cubes.astype(f32)
    for b in range(number):
        brick = features[0, 0, b]
        table[6 * b], table[6 * b + 1] = doubled(x_faces(brick.astype(f32)))
        sides = nt(brick, marks[...])
        table[6 * b + 2], table[6 * b + 3] = doubled(sides[:, :TILE])
        table[6 * b + 4], table[6 * b + 5] = doubled(sides[:, TILE:])
    for k, tile in enumerate(from_peers(received)):
        table[own + 2 * k], table[own + 2 * k + 1] = doubled(tile)
    copies[1].wait()
    table[own + 8] = jnp.zeros((channels, TILE), f32)

    fields[:channels] = cubes
    for axis in range(3):
        expanded = []
        for b in range(number):
            tile = jnp.where(half, table[links[0, 0, b, 2 * axis]], table[links[0, 0, b, 2 * axis + 1]])
            if axis == 0:
                gap = jnp.zeros((channels, voxels - 2 * TILE), f32)
                expanded.append(jnp.concatenate([tile, gap, tile], axis=1))
            else:
                expanded.append(nn(tile.astype(bf16), marks[TILE * (axis - 1):TILE * axis]))
        outer = jnp.concatenate(expanded, axis=1)
        low = jnp.where(coords[axis] == 0, outer, pltpu.roll(cubes32, strides[axis], 1))
        high = jnp.where(coords[axis] == EDGE - 1, outer, pltpu.roll(cubes32, total - strides[axis], 1))
        fields[channels * (2 * axis + 1):channels * (2 * axis + 2)] = low.astype(bf16)
        fields[channels * (2 * axis + 2):channels * (2 * axis + 3)] = high.astype(bf16)
    fields[depth:] = jnp.ones((PACK, total), bf16)

    copies[2].wait()
    copies[3].wait()
    first = bias[...].astype(bf16)
    rest = bias[...] - first.astype(f32)
    second = rest.astype(bf16)
    third = (rest - second.astype(f32)).astype(bf16)
    row = lax.broadcasted_iota(jnp.int32, (PACK, out_channels), 0)
    extra = jnp.where(row == 0, first.astype(f32),
                      jnp.where(row == 1, second.astype(f32), jnp.where(row == 2, third.astype(f32), 0.0)))
    taps[:depth] = weights[...]
    taps[depth:] = extra.astype(bf16)

    pre = tn(taps[...], fields[...])
    copies[4].wait()
    copies[5].wait()
    grad[out_channels:] = jnp.zeros((grad.shape[0] - out_channels, total), bf16)
    for b in range(number):
        part = pre[:, voxels * b:voxels * (b + 1)]
        s = jax.nn.sigmoid(part)
        value = upstream[0, 0, b].astype(f32) * (s * (1.0 + part * (1.0 - s)))
        grad[:out_channels, voxels * b:voxels * (b + 1)] = jnp.where(b < count[0, 0], value, 0.0).astype(bf16)

    found = nt(fields[...], grad[...])
    middle = depth // 2
    terms[:depth] = found[:depth, :TILE].astype(bf16)
    terms[depth:depth + middle] = (found[:middle, TILE:] + pltpu.roll(found[middle:depth, TILE:], LAYER, 1)).astype(bf16)
    row = lax.broadcasted_iota(jnp.int32, (PACK, TILE), 0)
    terms[depth + middle:] = jnp.where(row == 0, found[depth:, :TILE],
                                       jnp.where(row == 1, found[depth:, TILE:], 0.0)).astype(bf16)

    table_grad[...] = jnp.zeros(table_grad.shape, f32)
    live = grad[:out_channels]
    summed = nn(weights[:channels], live)
    for axis in range(3):
        low = nn(weights[channels * (2 * axis + 1):channels * (2 * axis + 2)], live)
        high = nn(weights[channels * (2 * axis + 2):channels * (2 * axis + 3)], live)
        at = coords[axis]
        summed = summed + jnp.where(at < EDGE - 1, pltpu.roll(low, total - strides[axis], 1), 0.0)
        summed = summed + jnp.where(at > 0, pltpu.roll(high, strides[axis], 1), 0.0)
        edge = jnp.where(at == 0, low, high)
        for b in range(number):
            brick = edge[:, voxels * b:voxels * (b + 1)]
            if axis == 0:
                tile = x_faces(brick)
            else:
                tile = nt(brick.astype(bf16), marks[TILE * (axis - 1):TILE * axis])
            to_low, to_high = doubled(tile)
            table_grad[links[0, 0, b, 2 * axis]] = to_low
            table_grad[links[0, 0, b, 2 * axis + 1]] = to_high
    low, high, cross_low, cross_high = [
        jnp.where(half, table_grad[own + 2 * k], table_grad[own + 2 * k + 1]) for k in range(4)]
    to_peers(sent, high, low, cross_high, cross_low)
    for b in range(number):
        parts = summed[:, voxels * b:voxels * (b + 1)]
        for axis in range(3):
            tile = jnp.where(half, table_grad[6 * b + 2 * axis], table_grad[6 * b + 2 * axis + 1])
            parts = parts + spread(tile, axis, marks, voxels)
        partial[:, voxels * b:voxels * (b + 1)] = parts


def spread(tile, axis, marks, voxels):
    if axis > 0:
        return nn(tile.astype(bf16), marks[TILE * (axis - 1):TILE * axis])
    half = low_half(tile.shape[0])
    gap = jnp.zeros((tile.shape[0], voxels - 2 * TILE), f32)
    return jnp.concatenate([jnp.where(half, tile, 0.0), gap, jnp.where(half, 0.0, tile)], axis=1)


def sum_chunks(arrived, shared, parts):
    rows = shared.shape[0] // parts
    value = jnp.sum(arrived[...].astype(f32).reshape(arrived.shape[0] // rows, rows, TILE), axis=0).astype(bf16)
    shared[...] = jnp.broadcast_to(value[None], (parts, rows, TILE)).reshape(shared.shape)


def finish_kernel(parts, partial, slab_in, cross_in, slab_far, slab_near, cross_far, cross_near, arrived, shared, result, marks, slab_list, cross_list, arrivals):
    copies = fetch((slab_in, cross_in), (slab_list, cross_list), arrivals)
    sum_chunks(arrived, shared, parts)
    number, channels, voxels = result.shape[2:]
    half = low_half(channels)
    marks[...] = layer_map(1, voxels)
    for copy in copies:
        copy.wait()
    second, first, cross_second, cross_first = from_peers((slab_far, slab_near, cross_far, cross_near))
    groups = ((slab_list, (first, second)), (cross_list, (cross_first, cross_second)))
    faces = [[doubled(back) for back in backs] for _, backs in groups]
    for b in range(number):
        parts = partial[:, voxels * b:voxels * (b + 1)]
        for axis, (listed, _) in enumerate(groups):
            sides = []
            for side in range(2):
                value = jnp.zeros((channels, TILE), f32)
                for k in range(2):
                    entry = listed[0, 0, 1 - side, k]
                    value = value + jnp.where(entry == 6 * b + 2 * axis + side, faces[axis][1 - side][k], 0.0)
                sides.append(value)
            parts = parts + spread(jnp.where(half, sides[0], sides[1]), axis, marks, voxels)
        result[0, 0, b] = parts.astype(bf16)


def unpack_kernel(scale, gathered, kernel_grad, bias_grad):
    taps, channels, out_channels = kernel_grad.shape
    depth = taps * channels
    middle = depth // 2
    wide = gathered[...].astype(f32) * scale
    rest = wide[depth:depth + middle]
    second = jnp.concatenate([rest, pltpu.roll(rest, LAYER, 1)], axis=0)
    for tap in range(taps):
        rows = slice(channels * tap, channels * (tap + 1))
        kernel_grad[tap, :, :TILE] = wide[rows]
        kernel_grad[tap, :, TILE:] = second[rows, :out_channels - TILE]
    bias_grad[:, :TILE] = wide[depth + middle:depth + middle + 1]
    bias_grad[:, TILE:] = wide[depth + middle + 1:depth + middle + 2, :out_channels - TILE]


def groups_of(bits, count):
    mask = sum(1 << bit for bit in bits)
    found = {}
    for device in range(count):
        found.setdefault(device & ~mask, []).append(device)
    return list(found.values())


def swap(slab_far, slab_near, cross_far, cross_near):
    def pairs(value, axis, first):
        lows = range(first, lax.axis_size(axis) - 1, 2)
        return lax.ppermute(value, axis, [pair for low in lows for pair in ((low, low + 1), (low + 1, low))])

    return (pairs(slab_far, "slab", 1), pairs(slab_near, "slab", 0),
            pairs(cross_far, "cross", 1), pairs(cross_near, "cross", 0))


def exchange(value, bits, count):
    return lax.all_to_all(value, ("slab", "cross"), 0, 0, axis_index_groups=groups_of(bits, count), tiled=True)


def shape(dims, dtype):
    return jax.ShapeDtypeStruct(dims, dtype)


def local(features, out_grad, weights, conv_bias, brick_count, neighbours, send_slab, send_cross):
    number, channels, voxels = features.shape[2:]
    out_channels = out_grad.shape[3]
    depth = 7 * channels
    total = number * voxels
    owners = lax.axis_size("slab") * lax.axis_size("cross")
    face_pair = shape((channels, TILE), bf16)
    limit = pltpu.CompilerParams(vmem_limit_bytes=FIRST)
    middle = pltpu.CompilerParams(vmem_limit_bytes=MIDDLE)
    small = pltpu.CompilerParams(vmem_limit_bytes=16 * 2**20)

    sends = pl.pallas_call(
        send_kernel,
        out_shape=[face_pair] * 4,
        in_specs=[HBM] * 3,
        out_specs=[VMEM] * 4,
        scratch_shapes=[
            pltpu.VMEM(features.shape, bf16),
            pltpu.SMEM(send_slab.shape, jnp.int32),
            pltpu.SMEM(send_cross.shape, jnp.int32),
            pltpu.SemaphoreType.DMA((3,)),
        ],
        compiler_params=limit,
    )(features, send_slab, send_cross)
    packed = shape((depth * 3 // 2 + PACK, TILE), bf16)
    *backs, terms, partial = pl.pallas_call(
        main_kernel,
        out_shape=[face_pair] * 4 + [packed, shape((channels, total), f32)],
        in_specs=[HBM] * 6 + [VMEM] * 4,
        out_specs=[VMEM] * 6,
        scratch_shapes=[
            pltpu.VMEM(features.shape, bf16),
            pltpu.VMEM((depth, out_channels), bf16),
            pltpu.VMEM(out_grad.shape, bf16),
            pltpu.VMEM((1, out_channels), f32),
            pltpu.SMEM(brick_count.shape, jnp.int32),
            pltpu.SMEM(neighbours.shape, jnp.int32),
            pltpu.VMEM((depth + PACK, total), bf16),
            pltpu.VMEM((2 * TILE, total), bf16),
            pltpu.VMEM((depth + PACK, out_channels), bf16),
            pltpu.VMEM((6 * number + 9, channels, TILE), f32),
            pltpu.VMEM((2 * TILE, voxels), bf16),
            pltpu.VMEM((6 * number + 9, channels, TILE), f32),
            pltpu.SemaphoreType.DMA((6,)),
        ],
        compiler_params=middle,
    )(features, weights.reshape(depth, out_channels), out_grad, conv_bias.reshape(1, out_channels), brick_count,
      neighbours, *swap(*sends))
    returned = swap(*backs)

    near = NEAR if owners == 512 else tuple(range(owners.bit_length() // 2))
    far = tuple(bit for bit in range(owners.bit_length() - 1) if bit not in near)
    arrived = exchange(terms, near, owners)
    shared = pl.pallas_call(
        lambda *refs: sum_chunks(*refs, 1 << len(far)),
        out_shape=shape((packed.shape[0] >> len(near) << len(far), TILE), bf16),
        in_specs=[VMEM], out_specs=VMEM, compiler_params=small,
    )(arrived)
    arrived = exchange(shared, far, owners)
    shared, grad_features = pl.pallas_call(
        lambda *refs: finish_kernel(1 << len(near), *refs),
        out_shape=[packed, shape(features.shape, bf16)],
        in_specs=[VMEM, HBM, HBM] + [VMEM] * 5,
        out_specs=[VMEM] * 2,
        scratch_shapes=[
            pltpu.VMEM((TILE, voxels), bf16),
            pltpu.SMEM(send_slab.shape, jnp.int32),
            pltpu.SMEM(send_cross.shape, jnp.int32),
            pltpu.SemaphoreType.DMA((2,)),
        ],
        compiler_params=small,
    )(partial, send_slab, send_cross, *returned, arrived)
    gathered = exchange(shared, near, owners)
    scale = 1.0 / math.sqrt(owners * total)
    kernel_grad, bias_grad = pl.pallas_call(
        lambda *refs: unpack_kernel(scale, *refs),
        out_shape=[shape(weights.shape, f32), shape((1, out_channels), f32)],
        in_specs=[VMEM],
        out_specs=[VMEM] * 2,
        compiler_params=small,
    )(gathered)
    return grad_features, kernel_grad, bias_grad.reshape(out_channels)


def solution(mesh):
    in_specs = (
        P("slab", "cross", None, None, None),
        P("slab", "cross", None, None, None),
        P(),
        P(),
        P("slab", "cross"),
        P("slab", "cross", None, None),
        P("slab", "cross", None, None),
        P("slab", "cross", None, None),
    )
    out_specs = (P("slab", "cross", None, None, None), P(), P())
    return jax.shard_map(local, mesh=mesh, in_specs=in_specs, out_specs=out_specs, check_vma=False)
```

```python
import math

import jax
import jax.numpy as jnp
from jax import lax
from jax.experimental import pallas as pl
from jax.experimental.pallas import tpu as pltpu
from jax.sharding import PartitionSpec as P

EDGE = 8
LAYER = EDGE * EDGE
TILE = 2 * LAYER
PACK = 16
FIRST = 60 * 2**20
MIDDLE = 55_700_000
NEAR = (0, 1, 2, 3, 6)
f32 = jnp.float32
bf16 = jnp.bfloat16
VMEM = pl.BlockSpec(memory_space=pltpu.VMEM)
SMEM = pl.BlockSpec(memory_space=pltpu.SMEM)
HBM = pl.BlockSpec(memory_space=pltpu.HBM)
ANY = pl.BlockSpec(memory_space=pl.ANY)


def nn(a, b):
    return lax.dot_general(a, b, (((1,), (0,)), ((), ())), preferred_element_type=f32)


def nt(a, b):
    return lax.dot_general(a, b, (((1,), (1,)), ((), ())), preferred_element_type=f32)


def tn(a, b):
    return lax.dot_general(a, b, (((0,), (0,)), ((), ())), preferred_element_type=f32)


def layer_map(axis, voxels):
    row = lax.broadcasted_iota(jnp.int32, (TILE, voxels), 0)
    v = lax.broadcasted_iota(jnp.int32, (TILE, voxels), 1)
    x, y, z = v >> 6, (v >> 3) & 7, v & 7
    along, beside = (y, x * EDGE + z) if axis == 1 else (z, x * EDGE + y)
    low = (along == 0) & (row == beside)
    high = (along == EDGE - 1) & (row == beside + LAYER)
    return jnp.where(low | high, 1.0, 0.0).astype(bf16)


def low_half(rows):
    return lax.broadcasted_iota(jnp.int32, (rows, TILE), 1) < LAYER


def x_faces(brick):
    return jnp.where(low_half(brick.shape[0]), brick[:, :TILE], brick[:, -TILE:])


def doubled(tile):
    turned = pltpu.roll(tile, LAYER, 1)
    half = low_half(tile.shape[0])
    return jnp.where(half, tile, turned), jnp.where(half, turned, tile)


def fetch(sources, targets, arrivals):
    copies = [pltpu.make_async_copy(a, b, arrivals.at[k]) for k, (a, b) in enumerate(zip(sources, targets))]
    for copy in copies:
        copy.start()
    return copies


def choose(axis, even, odd):
    return jnp.where((lax.axis_index(axis) & 1) == 0, even, odd)


def to_peers(refs, up, down, cross_up, cross_down):
    for ref, tile in zip(refs, (choose("slab", down, up), choose("slab", up, down),
                                choose("cross", cross_down, cross_up), choose("cross", cross_up, cross_down))):
        ref[...] = tile.astype(bf16)


def from_peers(refs):
    far, near, cross_far, cross_near = [ref[...].astype(f32) for ref in refs]
    return (choose("slab", far, near), choose("slab", near, far),
            choose("cross", cross_far, cross_near), choose("cross", cross_near, cross_far))


def send_kernel(features_in, slab_in, cross_in, *refs):
    faces, (features, slab_list, cross_list, arrivals) = refs[:4], refs[4:]
    copies = fetch((features_in, slab_in, cross_in), (features, slab_list, cross_list), arrivals)
    number, channels, voxels = features.shape[2:]
    y_map = layer_map(1, voxels)
    for copy in copies:
        copy.wait()
    half = low_half(channels)
    tables = ([], [])
    for b in range(number):
        brick = features[0, 0, b]
        tables[0].append(doubled(x_faces(brick.astype(f32))))
        tables[1].append(doubled(nt(brick, y_map)))
    sends = []
    for axis, listed in enumerate((slab_list, cross_list)):
        for row in range(2):
            side = 1 - row
            picked = []
            for k in range(2):
                entry = listed[0, 0, row, k]
                value = jnp.zeros((channels, TILE), f32)
                for b in range(number):
                    value = jnp.where(entry == 6 * b + 2 * axis + side, tables[axis][b][side], value)
                picked.append(value)
            sends.append(jnp.where(half, picked[0], picked[1]))
    to_peers(faces, *sends)


def main_kernel(features_in, weights_in, upstream_in, bias_in, count_in, links_in, *refs):
    received, (terms, grad), refs = refs[:4], refs[4:6], refs[6:]
    features, weights, upstream, bias, count, links, fields, taps, table, marks, arrivals = refs
    copies = fetch(
        (features_in, links_in, weights_in, bias_in, count_in, upstream_in),
        (features, links, weights, bias, count, upstream), arrivals)
    number, channels, voxels = features.shape[2:]
    out_channels = upstream.shape[3]
    depth = 7 * channels
    total = number * voxels
    own = 6 * number
    half = low_half(channels)
    lane = lax.broadcasted_iota(jnp.int32, (channels, total), 1)
    v = lane & (voxels - 1)
    coords = (v >> 6, (v >> 3) & 7, v & 7)
    strides = (LAYER, EDGE, 1)
    for axis in (1, 2):
        marks[TILE * (axis - 1):TILE * axis] = layer_map(axis, voxels)
    copies[0].wait()

    cubes = jnp.concatenate([features[0, 0, b] for b in range(number)], axis=1)
    cubes32 = cubes.astype(f32)
    for b in range(number):
        brick = features[0, 0, b]
        table[6 * b], table[6 * b + 1] = doubled(x_faces(brick.astype(f32)))
        sides = nt(brick, marks[...])
        table[6 * b + 2], table[6 * b + 3] = doubled(sides[:, :TILE])
        table[6 * b + 4], table[6 * b + 5] = doubled(sides[:, TILE:])
    for k, tile in enumerate(from_peers(received)):
        table[own + 2 * k], table[own + 2 * k + 1] = doubled(tile)
    copies[1].wait()
    table[own + 8] = jnp.zeros((channels, TILE), f32)

    fields[:channels] = cubes
    for axis in range(3):
        expanded = []
        for b in range(number):
            tile = jnp.where(half, table[links[0, 0, b, 2 * axis]], table[links[0, 0, b, 2 * axis + 1]])
            if axis == 0:
                gap = jnp.zeros((channels, voxels - 2 * TILE), f32)
                expanded.append(jnp.concatenate([tile, gap, tile], axis=1))
            else:
                expanded.append(nn(tile.astype(bf16), marks[TILE * (axis - 1):TILE * axis]))
        outer = jnp.concatenate(expanded, axis=1)
        low = jnp.where(coords[axis] == 0, outer, pltpu.roll(cubes32, strides[axis], 1))
        high = jnp.where(coords[axis] == EDGE - 1, outer, pltpu.roll(cubes32, total - strides[axis], 1))
        fields[channels * (2 * axis + 1):channels * (2 * axis + 2)] = low.astype(bf16)
        fields[channels * (2 * axis + 2):channels * (2 * axis + 3)] = high.astype(bf16)
    fields[depth:] = jnp.ones((PACK, total), bf16)

    copies[2].wait()
    copies[3].wait()
    first = bias[...].astype(bf16)
    rest = bias[...] - first.astype(f32)
    second = rest.astype(bf16)
    third = (rest - second.astype(f32)).astype(bf16)
    row = lax.broadcasted_iota(jnp.int32, (PACK, out_channels), 0)
    extra = jnp.where(row == 0, first.astype(f32),
                      jnp.where(row == 1, second.astype(f32), jnp.where(row == 2, third.astype(f32), 0.0)))
    taps[:depth] = weights[...]
    taps[depth:] = extra.astype(bf16)

    pre = tn(taps[...], fields[...])
    copies[4].wait()
    copies[5].wait()
    grad[out_channels:] = jnp.zeros((grad.shape[0] - out_channels, total), bf16)
    for b in range(number):
        part = pre[:, voxels * b:voxels * (b + 1)]
        s = jax.nn.sigmoid(part)
        value = upstream[0, 0, b].astype(f32) * (s * (1.0 + part * (1.0 - s)))
        grad[:out_channels, voxels * b:voxels * (b + 1)] = jnp.where(b < count[0, 0], value, 0.0).astype(bf16)

    found = nt(fields[...], grad[...])
    middle = depth // 2
    terms[:depth] = found[:depth, :TILE].astype(bf16)
    terms[depth:depth + middle] = (found[:middle, TILE:] + pltpu.roll(found[middle:depth, TILE:], LAYER, 1)).astype(bf16)
    row = lax.broadcasted_iota(jnp.int32, (PACK, TILE), 0)
    terms[depth + middle:] = jnp.where(row == 0, found[depth:, :TILE],
                                       jnp.where(row == 1, found[depth:, TILE:], 0.0)).astype(bf16)


def back_kernel(weights, grad, links_in, *refs):
    sent, (partial, marks, table_grad, links, arrivals) = refs[:4], refs[4:]
    copies = fetch((links_in,), (links,), arrivals)
    channels, total = partial.shape
    number = links.shape[2]
    voxels = total // number
    out_channels = weights.shape[1]
    own = 6 * number
    half = low_half(channels)
    v = lax.broadcasted_iota(jnp.int32, (channels, total), 1) & (voxels - 1)
    coords = (v >> 6, (v >> 3) & 7, v & 7)
    strides = (LAYER, EDGE, 1)
    for axis in (1, 2):
        marks[TILE * (axis - 1):TILE * axis] = layer_map(axis, voxels)
    table_grad[...] = jnp.zeros(table_grad.shape, f32)
    copies[0].wait()
    live = grad[:out_channels]
    summed = nn(weights[:channels], live)
    for axis in range(3):
        low = nn(weights[channels * (2 * axis + 1):channels * (2 * axis + 2)], live)
        high = nn(weights[channels * (2 * axis + 2):channels * (2 * axis + 3)], live)
        at = coords[axis]
        summed = summed + jnp.where(at < EDGE - 1, pltpu.roll(low, total - strides[axis], 1), 0.0)
        summed = summed + jnp.where(at > 0, pltpu.roll(high, strides[axis], 1), 0.0)
        edge = jnp.where(at == 0, low, high)
        for b in range(number):
            brick = edge[:, voxels * b:voxels * (b + 1)]
            if axis == 0:
                tile = x_faces(brick)
            else:
                tile = nt(brick.astype(bf16), marks[TILE * (axis - 1):TILE * axis])
            to_low, to_high = doubled(tile)
            table_grad[links[0, 0, b, 2 * axis]] = to_low
            table_grad[links[0, 0, b, 2 * axis + 1]] = to_high
    low, high, cross_low, cross_high = [
        jnp.where(half, table_grad[own + 2 * k], table_grad[own + 2 * k + 1]) for k in range(4)]
    to_peers(sent, high, low, cross_high, cross_low)
    for b in range(number):
        parts = summed[:, voxels * b:voxels * (b + 1)]
        for axis in range(3):
            tile = jnp.where(half, table_grad[6 * b + 2 * axis], table_grad[6 * b + 2 * axis + 1])
            parts = parts + spread(tile, axis, marks, voxels)
        partial[:, voxels * b:voxels * (b + 1)] = parts


def spread(tile, axis, marks, voxels):
    if axis > 0:
        return nn(tile.astype(bf16), marks[TILE * (axis - 1):TILE * axis])
    half = low_half(tile.shape[0])
    gap = jnp.zeros((tile.shape[0], voxels - 2 * TILE), f32)
    return jnp.concatenate([jnp.where(half, tile, 0.0), gap, jnp.where(half, 0.0, tile)], axis=1)


def sum_chunks(arrived, shared, parts):
    rows = shared.shape[0] // parts
    value = jnp.sum(arrived[...].astype(f32).reshape(arrived.shape[0] // rows, rows, TILE), axis=0).astype(bf16)
    shared[...] = jnp.broadcast_to(value[None], (parts, rows, TILE)).reshape(shared.shape)


def finish_kernel(partial, slab_in, cross_in, slab_far, slab_near, cross_far, cross_near, result, marks, slab_list,
                  cross_list, arrivals):
    copies = fetch((slab_in, cross_in), (slab_list, cross_list), arrivals)
    number, channels, voxels = result.shape[2:]
    half = low_half(channels)
    marks[...] = layer_map(1, voxels)
    for copy in copies:
        copy.wait()
    second, first, cross_second, cross_first = from_peers((slab_far, slab_near, cross_far, cross_near))
    groups = ((slab_list, (first, second)), (cross_list, (cross_first, cross_second)))
    faces = [[doubled(back) for back in backs] for _, backs in groups]
    for b in range(number):
        parts = partial[:, voxels * b:voxels * (b + 1)]
        for axis, (listed, _) in enumerate(groups):
            sides = []
            for side in range(2):
                value = jnp.zeros((channels, TILE), f32)
                for k in range(2):
                    entry = listed[0, 0, 1 - side, k]
                    value = value + jnp.where(entry == 6 * b + 2 * axis + side, faces[axis][1 - side][k], 0.0)
                sides.append(value)
            parts = parts + spread(jnp.where(half, sides[0], sides[1]), axis, marks, voxels)
        result[0, 0, b] = parts.astype(bf16)


def unpack_kernel(scale, gathered, kernel_grad, bias_grad):
    taps, channels, out_channels = kernel_grad.shape
    depth = taps * channels
    middle = depth // 2
    wide = gathered[...].astype(f32) * scale
    rest = wide[depth:depth + middle]
    second = jnp.concatenate([rest, pltpu.roll(rest, LAYER, 1)], axis=0)
    for tap in range(taps):
        rows = slice(channels * tap, channels * (tap + 1))
        kernel_grad[tap, :, :TILE] = wide[rows]
        kernel_grad[tap, :, TILE:] = second[rows, :out_channels - TILE]
    bias_grad[:, :TILE] = wide[depth + middle:depth + middle + 1]
    bias_grad[:, TILE:] = wide[depth + middle + 1:depth + middle + 2, :out_channels - TILE]


def groups_of(bits, count):
    mask = sum(1 << bit for bit in bits)
    found = {}
    for device in range(count):
        found.setdefault(device & ~mask, []).append(device)
    return list(found.values())


def swap(far, near, axis):
    def pairs(value, first):
        lows = range(first, lax.axis_size(axis) - 1, 2)
        return lax.ppermute(value, axis, [pair for low in lows for pair in ((low, low + 1), (low + 1, low))])

    return pairs(far, 1), pairs(near, 0)


def staged_sum(arrived, rows, parts, ended, passed, params):
    shared, *passed = pl.pallas_call(
        lambda arrived, *refs: sum_chunks(arrived, refs[len(ended) + len(passed)], parts),
        out_shape=[shape((rows, TILE), bf16)] + [shape(x.shape, x.dtype) for x in passed],
        in_specs=[VMEM] + [ANY] * (len(ended) + len(passed)),
        out_specs=[VMEM] + [ANY] * len(passed),
        input_output_aliases={1 + len(ended) + k: 1 + k for k in range(len(passed))},
        compiler_params=params,
    )(arrived, *ended, *passed)
    return shared, passed


def exchange(value, bits, count):
    return lax.all_to_all(value, ("slab", "cross"), 0, 0, axis_index_groups=groups_of(bits, count), tiled=True)


def shape(dims, dtype):
    return jax.ShapeDtypeStruct(dims, dtype)


def local(features, out_grad, weights, conv_bias, brick_count, neighbours, send_slab, send_cross):
    number, channels, voxels = features.shape[2:]
    out_channels = out_grad.shape[3]
    depth = 7 * channels
    total = number * voxels
    owners = lax.axis_size("slab") * lax.axis_size("cross")
    face_pair = shape((channels, TILE), bf16)
    limit = pltpu.CompilerParams(vmem_limit_bytes=FIRST)
    middle = pltpu.CompilerParams(vmem_limit_bytes=MIDDLE)
    small = pltpu.CompilerParams(vmem_limit_bytes=16 * 2**20)

    sends = pl.pallas_call(
        send_kernel,
        out_shape=[face_pair] * 4,
        in_specs=[HBM] * 3,
        out_specs=[VMEM] * 4,
        scratch_shapes=[
            pltpu.VMEM(features.shape, bf16),
            pltpu.SMEM(send_slab.shape, jnp.int32),
            pltpu.SMEM(send_cross.shape, jnp.int32),
            pltpu.SemaphoreType.DMA((3,)),
        ],
        compiler_params=limit,
    )(features, send_slab, send_cross)
    packed = shape((depth * 3 // 2 + PACK, TILE), bf16)
    terms, grad = pl.pallas_call(
        main_kernel,
        out_shape=[packed, shape((2 * TILE, total), bf16)],
        in_specs=[HBM] * 6 + [VMEM] * 4,
        out_specs=[VMEM] * 2,
        scratch_shapes=[
            pltpu.VMEM(features.shape, bf16),
            pltpu.VMEM((depth, out_channels), bf16),
            pltpu.VMEM(out_grad.shape, bf16),
            pltpu.VMEM((1, out_channels), f32),
            pltpu.SMEM(brick_count.shape, jnp.int32),
            pltpu.SMEM(neighbours.shape, jnp.int32),
            pltpu.VMEM((depth + PACK, total), bf16),
            pltpu.VMEM((depth + PACK, out_channels), bf16),
            pltpu.VMEM((6 * number + 9, channels, TILE), f32),
            pltpu.VMEM((2 * TILE, voxels), bf16),
            pltpu.SemaphoreType.DMA((6,)),
        ],
        compiler_params=middle,
    )(features, weights.reshape(depth, out_channels), out_grad, conv_bias.reshape(1, out_channels), brick_count,
      neighbours, *swap(*sends[:2], "slab"), *swap(*sends[2:], "cross"))
    *backs, partial = pl.pallas_call(
        back_kernel,
        out_shape=[face_pair] * 4 + [shape((channels, total), f32)],
        in_specs=[VMEM, VMEM, HBM],
        out_specs=[VMEM] * 5,
        scratch_shapes=[
            pltpu.VMEM((2 * TILE, voxels), bf16),
            pltpu.VMEM((6 * number + 9, channels, TILE), f32),
            pltpu.SMEM(neighbours.shape, jnp.int32),
            pltpu.SemaphoreType.DMA((1,)),
        ],
        compiler_params=small,
    )(weights.reshape(depth, out_channels), grad, neighbours)

    near = NEAR if owners == 512 else tuple(range(owners.bit_length() // 2))
    far = tuple(bit for bit in range(owners.bit_length() - 1) if bit not in near)
    arrived = exchange(terms, near, owners)
    shared, slab_back = staged_sum(
        arrived, packed.shape[0] >> len(near) << len(far), 1 << len(far), [], backs[:2], small)
    arrived = exchange(shared, far, owners)
    slab_back = swap(*slab_back, "slab")
    shared, passed = staged_sum(
        arrived, packed.shape[0], 1 << len(near), slab_back, [partial, *backs[2:]], small)
    partial, cross_back = passed[0], swap(*passed[1:], "cross")
    grad_features = pl.pallas_call(
        finish_kernel,
        out_shape=shape(features.shape, bf16),
        in_specs=[VMEM, HBM, HBM] + [VMEM] * 4,
        out_specs=VMEM,
        scratch_shapes=[
            pltpu.VMEM((TILE, voxels), bf16),
            pltpu.SMEM(send_slab.shape, jnp.int32),
            pltpu.SMEM(send_cross.shape, jnp.int32),
            pltpu.SemaphoreType.DMA((2,)),
        ],
        compiler_params=small,
    )(partial, send_slab, send_cross, *slab_back, *cross_back)
    gathered = exchange(shared, near, owners)
    scale = 1.0 / math.sqrt(owners * total)
    kernel_grad, bias_grad = pl.pallas_call(
        lambda *refs: unpack_kernel(scale, *refs),
        out_shape=[shape(weights.shape, f32), shape((1, out_channels), f32)],
        in_specs=[VMEM],
        out_specs=[VMEM] * 2,
        compiler_params=small,
    )(gathered)
    return grad_features, kernel_grad, bias_grad.reshape(out_channels)


def solution(mesh):
    in_specs = (
        P("slab", "cross", None, None, None),
        P("slab", "cross", None, None, None),
        P(),
        P(),
        P("slab", "cross"),
        P("slab", "cross", None, None),
        P("slab", "cross", None, None),
        P("slab", "cross", None, None),
    )
    out_specs = (P("slab", "cross", None, None, None), P(), P())
    return jax.shard_map(local, mesh=mesh, in_specs=in_specs, out_specs=out_specs, check_vma=False)
```

```python
import math

import jax
import jax.numpy as jnp
from jax import lax
from jax.experimental import pallas as pl
from jax.experimental.pallas import tpu as pltpu
from jax.sharding import PartitionSpec as P

EDGE = 8
LAYER = EDGE * EDGE
TILE = 2 * LAYER
PACK = 16
FIRST = 60 * 2**20
MIDDLE = 55_700_000
NEAR = (0, 1, 2, 3, 6)
f32 = jnp.float32
bf16 = jnp.bfloat16
VMEM = pl.BlockSpec(memory_space=pltpu.VMEM)
SMEM = pl.BlockSpec(memory_space=pltpu.SMEM)
HBM = pl.BlockSpec(memory_space=pltpu.HBM)
ANY = pl.BlockSpec(memory_space=pl.ANY)


def nn(a, b):
    return lax.dot_general(a, b, (((1,), (0,)), ((), ())), preferred_element_type=f32)


def nt(a, b):
    return lax.dot_general(a, b, (((1,), (1,)), ((), ())), preferred_element_type=f32)


def tn(a, b):
    return lax.dot_general(a, b, (((0,), (0,)), ((), ())), preferred_element_type=f32)


def layer_map(axis, voxels):
    row = lax.broadcasted_iota(jnp.int32, (TILE, voxels), 0)
    v = lax.broadcasted_iota(jnp.int32, (TILE, voxels), 1)
    x, y, z = v >> 6, (v >> 3) & 7, v & 7
    along, beside = (y, x * EDGE + z) if axis == 1 else (z, x * EDGE + y)
    low = (along == 0) & (row == beside)
    high = (along == EDGE - 1) & (row == beside + LAYER)
    return jnp.where(low | high, 1.0, 0.0).astype(bf16)


def low_half(rows):
    return lax.broadcasted_iota(jnp.int32, (rows, TILE), 1) < LAYER


def x_faces(brick):
    return jnp.where(low_half(brick.shape[0]), brick[:, :TILE], brick[:, -TILE:])


def doubled(tile):
    turned = pltpu.roll(tile, LAYER, 1)
    half = low_half(tile.shape[0])
    return jnp.where(half, tile, turned), jnp.where(half, turned, tile)


def fetch(sources, targets, arrivals):
    copies = [pltpu.make_async_copy(a, b, arrivals.at[k]) for k, (a, b) in enumerate(zip(sources, targets))]
    for copy in copies:
        copy.start()
    return copies


def choose(axis, even, odd):
    return jnp.where((lax.axis_index(axis) & 1) == 0, even, odd)


def to_peers(refs, up, down, cross_up, cross_down):
    for ref, tile in zip(refs, (choose("slab", down, up), choose("slab", up, down),
                                choose("cross", cross_down, cross_up), choose("cross", cross_up, cross_down))):
        ref[...] = tile.astype(bf16)


def from_peers(refs):
    far, near, cross_far, cross_near = [ref[...].astype(f32) for ref in refs]
    return (choose("slab", far, near), choose("slab", near, far),
            choose("cross", cross_far, cross_near), choose("cross", cross_near, cross_far))


def send_kernel(features_in, slab_in, cross_in, *refs):
    faces, (features, slab_list, cross_list, arrivals) = refs[:4], refs[4:]
    copies = fetch((features_in, slab_in, cross_in), (features, slab_list, cross_list), arrivals)
    number, channels, voxels = features.shape[2:]
    y_map = layer_map(1, voxels)
    for copy in copies:
        copy.wait()
    half = low_half(channels)
    tables = ([], [])
    for b in range(number):
        brick = features[0, 0, b]
        tables[0].append(doubled(x_faces(brick.astype(f32))))
        tables[1].append(doubled(nt(brick, y_map)))
    sends = []
    for axis, listed in enumerate((slab_list, cross_list)):
        for row in range(2):
            side = 1 - row
            picked = []
            for k in range(2):
                entry = listed[0, 0, row, k]
                value = jnp.zeros((channels, TILE), f32)
                for b in range(number):
                    value = jnp.where(entry == 6 * b + 2 * axis + side, tables[axis][b][side], value)
                picked.append(value)
            sends.append(jnp.where(half, picked[0], picked[1]))
    to_peers(faces, *sends)


def main_kernel(features_in, weights_in, upstream_in, bias_in, count_in, links_in, *refs):
    received, (terms, grad), refs = refs[:4], refs[4:6], refs[6:]
    features, weights, upstream, bias, count, links, fields, taps, table, marks, arrivals = refs
    copies = fetch(
        (features_in, links_in, weights_in, bias_in, count_in, upstream_in),
        (features, links, weights, bias, count, upstream), arrivals)
    number, channels, voxels = features.shape[2:]
    out_channels = upstream.shape[3]
    depth = 7 * channels
    total = number * voxels
    own = 6 * number
    half = low_half(channels)
    lane = lax.broadcasted_iota(jnp.int32, (channels, total), 1)
    v = lane & (voxels - 1)
    coords = (v >> 6, (v >> 3) & 7, v & 7)
    strides = (LAYER, EDGE, 1)
    for axis in (1, 2):
        marks[TILE * (axis - 1):TILE * axis] = layer_map(axis, voxels)
    copies[0].wait()

    cubes = jnp.concatenate([features[0, 0, b] for b in range(number)], axis=1)
    cubes32 = cubes.astype(f32)
    for b in range(number):
        brick = features[0, 0, b]
        table[6 * b], table[6 * b + 1] = doubled(x_faces(brick.astype(f32)))
        sides = nt(brick, marks[...])
        table[6 * b + 2], table[6 * b + 3] = doubled(sides[:, :TILE])
        table[6 * b + 4], table[6 * b + 5] = doubled(sides[:, TILE:])
    for k, tile in enumerate(from_peers(received)):
        table[own + 2 * k], table[own + 2 * k + 1] = doubled(tile)
    copies[1].wait()
    table[own + 8] = jnp.zeros((channels, TILE), f32)

    fields[:channels] = cubes
    for axis in range(3):
        expanded = []
        for b in range(number):
            tile = jnp.where(half, table[links[0, 0, b, 2 * axis]], table[links[0, 0, b, 2 * axis + 1]])
            if axis == 0:
                gap = jnp.zeros((channels, voxels - 2 * TILE), f32)
                expanded.append(jnp.concatenate([tile, gap, tile], axis=1))
            else:
                expanded.append(nn(tile.astype(bf16), marks[TILE * (axis - 1):TILE * axis]))
        outer = jnp.concatenate(expanded, axis=1)
        low = jnp.where(coords[axis] == 0, outer, pltpu.roll(cubes32, strides[axis], 1))
        high = jnp.where(coords[axis] == EDGE - 1, outer, pltpu.roll(cubes32, total - strides[axis], 1))
        fields[channels * (2 * axis + 1):channels * (2 * axis + 2)] = low.astype(bf16)
        fields[channels * (2 * axis + 2):channels * (2 * axis + 3)] = high.astype(bf16)
    fields[depth:] = jnp.ones((PACK, total), bf16)

    copies[2].wait()
    copies[3].wait()
    first = bias[...].astype(bf16)
    rest = bias[...] - first.astype(f32)
    second = rest.astype(bf16)
    third = (rest - second.astype(f32)).astype(bf16)
    row = lax.broadcasted_iota(jnp.int32, (PACK, out_channels), 0)
    extra = jnp.where(row == 0, first.astype(f32),
                      jnp.where(row == 1, second.astype(f32), jnp.where(row == 2, third.astype(f32), 0.0)))
    taps[:depth] = weights[...]
    taps[depth:] = extra.astype(bf16)

    pre = tn(taps[...], fields[...])
    copies[4].wait()
    copies[5].wait()
    grad[out_channels:] = jnp.zeros((grad.shape[0] - out_channels, total), bf16)
    for b in range(number):
        part = pre[:, voxels * b:voxels * (b + 1)]
        s = jax.nn.sigmoid(part)
        value = upstream[0, 0, b].astype(f32) * (s * (1.0 + part * (1.0 - s)))
        grad[:out_channels, voxels * b:voxels * (b + 1)] = jnp.where(b < count[0, 0], value, 0.0).astype(bf16)

    found = nt(fields[...], grad[...])
    middle = depth // 2
    terms[:depth] = found[:depth, :TILE].astype(bf16)
    terms[depth:depth + middle] = (found[:middle, TILE:] + pltpu.roll(found[middle:depth, TILE:], LAYER, 1)).astype(bf16)
    row = lax.broadcasted_iota(jnp.int32, (PACK, TILE), 0)
    terms[depth + middle:] = jnp.where(row == 0, found[depth:, :TILE],
                                       jnp.where(row == 1, found[depth:, TILE:], 0.0)).astype(bf16)


def list_places(number):
    return [(axis, side, b, place) for axis in range(2) for side in range(2) for b in range(number) for place in range(2)]


def back_kernel(weights, grad, links_in, slab_in, cross_in, *refs):
    sent, (partial, flags, marks, table_grad, links, slab_list, cross_list, arrivals) = refs[:4], refs[4:]
    copies = fetch((links_in, slab_in, cross_in), (links, slab_list, cross_list), arrivals)
    channels, total = partial.shape
    number = links.shape[2]
    voxels = total // number
    out_channels = weights.shape[1]
    own = 6 * number
    half = low_half(channels)
    v = lax.broadcasted_iota(jnp.int32, (channels, total), 1) & (voxels - 1)
    coords = (v >> 6, (v >> 3) & 7, v & 7)
    strides = (LAYER, EDGE, 1)
    for axis in (1, 2):
        marks[TILE * (axis - 1):TILE * axis] = layer_map(axis, voxels)
    table_grad[...] = jnp.zeros(table_grad.shape, f32)
    for copy in copies:
        copy.wait()
    row = lax.broadcasted_iota(jnp.int32, flags.shape, 0)
    named = jnp.zeros(flags.shape, f32)
    for k, (axis, side, b, place) in enumerate(list_places(number)):
        entry = (slab_list, cross_list)[axis][0, 0, 1 - side, place]
        named = jnp.where((row == k) & (entry == 6 * b + 2 * axis + side), 1.0, named)
    flags[...] = named
    live = grad[:out_channels]
    summed = nn(weights[:channels], live)
    for axis in range(3):
        low = nn(weights[channels * (2 * axis + 1):channels * (2 * axis + 2)], live)
        high = nn(weights[channels * (2 * axis + 2):channels * (2 * axis + 3)], live)
        at = coords[axis]
        summed = summed + jnp.where(at < EDGE - 1, pltpu.roll(low, total - strides[axis], 1), 0.0)
        summed = summed + jnp.where(at > 0, pltpu.roll(high, strides[axis], 1), 0.0)
        edge = jnp.where(at == 0, low, high)
        for b in range(number):
            brick = edge[:, voxels * b:voxels * (b + 1)]
            if axis == 0:
                tile = x_faces(brick)
            else:
                tile = nt(brick.astype(bf16), marks[TILE * (axis - 1):TILE * axis])
            to_low, to_high = doubled(tile)
            table_grad[links[0, 0, b, 2 * axis]] = to_low
            table_grad[links[0, 0, b, 2 * axis + 1]] = to_high
    low, high, cross_low, cross_high = [
        jnp.where(half, table_grad[own + 2 * k], table_grad[own + 2 * k + 1]) for k in range(4)]
    to_peers(sent, high, low, cross_high, cross_low)
    for b in range(number):
        parts = summed[:, voxels * b:voxels * (b + 1)]
        for axis in range(3):
            tile = jnp.where(half, table_grad[6 * b + 2 * axis], table_grad[6 * b + 2 * axis + 1])
            parts = parts + spread(tile, axis, marks, voxels)
        partial[:, voxels * b:voxels * (b + 1)] = parts


def spread(tile, axis, marks, voxels):
    if axis > 0:
        return nn(tile.astype(bf16), marks[TILE * (axis - 1):TILE * axis])
    half = low_half(tile.shape[0])
    gap = jnp.zeros((tile.shape[0], voxels - 2 * TILE), f32)
    return jnp.concatenate([jnp.where(half, tile, 0.0), gap, jnp.where(half, 0.0, tile)], axis=1)


def sum_chunks(arrived, shared, parts):
    rows = shared.shape[0] // parts
    value = jnp.sum(arrived[...].astype(f32).reshape(arrived.shape[0] // rows, rows, TILE), axis=0).astype(bf16)
    shared[...] = jnp.broadcast_to(value[None], (parts, rows, TILE)).reshape(shared.shape)


def finish_kernel(scale, gathered, partial, flags, slab_far, slab_near, cross_far, cross_near,
                  kernel_grad, bias_grad, result, marks):
    unpack(scale, gathered, kernel_grad, bias_grad)
    number, channels, voxels = result.shape[2:]
    half = low_half(channels)
    marks[...] = layer_map(1, voxels)
    second, first, cross_second, cross_first = from_peers((slab_far, slab_near, cross_far, cross_near))
    faces = [[doubled(back) for back in backs] for backs in ((second, first), (cross_second, cross_first))]
    sides = {}
    for k, (axis, side, b, place) in enumerate(list_places(number)):
        value = flags[k:k + 1] * faces[axis][side][place]
        sides[axis, side, b] = sides[axis, side, b] + value if place else value
    for b in range(number):
        parts = partial[:, voxels * b:voxels * (b + 1)]
        for axis in range(2):
            parts = parts + spread(jnp.where(half, sides[axis, 0, b], sides[axis, 1, b]), axis, marks, voxels)
        result[0, 0, b] = parts.astype(bf16)


def unpack(scale, gathered, kernel_grad, bias_grad):
    taps, channels, out_channels = kernel_grad.shape
    depth = taps * channels
    middle = depth // 2
    wide = gathered[...].astype(f32) * scale
    rest = wide[depth:depth + middle]
    second = jnp.concatenate([rest, pltpu.roll(rest, LAYER, 1)], axis=0)
    for tap in range(taps):
        rows = slice(channels * tap, channels * (tap + 1))
        kernel_grad[tap, :, :TILE] = wide[rows]
        kernel_grad[tap, :, TILE:] = second[rows, :out_channels - TILE]
    bias_grad[:, :TILE] = wide[depth + middle:depth + middle + 1]
    bias_grad[:, TILE:] = wide[depth + middle + 1:depth + middle + 2, :out_channels - TILE]


def groups_of(bits, count):
    mask = sum(1 << bit for bit in bits)
    found = {}
    for device in range(count):
        found.setdefault(device & ~mask, []).append(device)
    return list(found.values())


def swap(far, near, axis):
    def pairs(value, first):
        lows = range(first, lax.axis_size(axis) - 1, 2)
        return lax.ppermute(value, axis, [pair for low in lows for pair in ((low, low + 1), (low + 1, low))])

    return pairs(far, 1), pairs(near, 0)


def staged_sum(arrived, rows, parts, ended, passed, params):
    shared, *passed = pl.pallas_call(
        lambda arrived, *refs: sum_chunks(arrived, refs[len(ended) + len(passed)], parts),
        out_shape=[shape((rows, TILE), bf16)] + [shape(x.shape, x.dtype) for x in passed],
        in_specs=[VMEM] + [ANY] * (len(ended) + len(passed)),
        out_specs=[VMEM] + [ANY] * len(passed),
        input_output_aliases={1 + len(ended) + k: 1 + k for k in range(len(passed))},
        compiler_params=params,
    )(arrived, *ended, *passed)
    return shared, passed


def exchange(value, bits, count):
    return lax.all_to_all(value, ("slab", "cross"), 0, 0, axis_index_groups=groups_of(bits, count), tiled=True)


def shape(dims, dtype):
    return jax.ShapeDtypeStruct(dims, dtype)


def local(features, out_grad, weights, conv_bias, brick_count, neighbours, send_slab, send_cross):
    number, channels, voxels = features.shape[2:]
    out_channels = out_grad.shape[3]
    depth = 7 * channels
    total = number * voxels
    owners = lax.axis_size("slab") * lax.axis_size("cross")
    face_pair = shape((channels, TILE), bf16)
    limit = pltpu.CompilerParams(vmem_limit_bytes=FIRST)
    middle = pltpu.CompilerParams(vmem_limit_bytes=MIDDLE)
    small = pltpu.CompilerParams(vmem_limit_bytes=16 * 2**20)

    sends = pl.pallas_call(
        send_kernel,
        out_shape=[face_pair] * 4,
        in_specs=[HBM] * 3,
        out_specs=[VMEM] * 4,
        scratch_shapes=[
            pltpu.VMEM(features.shape, bf16),
            pltpu.SMEM(send_slab.shape, jnp.int32),
            pltpu.SMEM(send_cross.shape, jnp.int32),
            pltpu.SemaphoreType.DMA((3,)),
        ],
        compiler_params=limit,
    )(features, send_slab, send_cross)
    packed = shape((depth * 3 // 2 + PACK, TILE), bf16)
    terms, grad = pl.pallas_call(
        main_kernel,
        out_shape=[packed, shape((2 * TILE, total), bf16)],
        in_specs=[HBM] * 6 + [VMEM] * 4,
        out_specs=[VMEM] * 2,
        scratch_shapes=[
            pltpu.VMEM(features.shape, bf16),
            pltpu.VMEM((depth, out_channels), bf16),
            pltpu.VMEM(out_grad.shape, bf16),
            pltpu.VMEM((1, out_channels), f32),
            pltpu.SMEM(brick_count.shape, jnp.int32),
            pltpu.SMEM(neighbours.shape, jnp.int32),
            pltpu.VMEM((depth + PACK, total), bf16),
            pltpu.VMEM((depth + PACK, out_channels), bf16),
            pltpu.VMEM((6 * number + 9, channels, TILE), f32),
            pltpu.VMEM((2 * TILE, voxels), bf16),
            pltpu.SemaphoreType.DMA((6,)),
        ],
        compiler_params=middle,
    )(features, weights.reshape(depth, out_channels), out_grad, conv_bias.reshape(1, out_channels), brick_count,
      neighbours, *swap(*sends[:2], "slab"), *swap(*sends[2:], "cross"))
    *backs, partial, flags = pl.pallas_call(
        back_kernel,
        out_shape=[face_pair] * 4 + [shape((channels, total), f32), shape((len(list_places(number)), TILE), f32)],
        in_specs=[VMEM, VMEM] + [HBM] * 3,
        out_specs=[VMEM] * 6,
        scratch_shapes=[
            pltpu.VMEM((2 * TILE, voxels), bf16),
            pltpu.VMEM((6 * number + 9, channels, TILE), f32),
            pltpu.SMEM(neighbours.shape, jnp.int32),
            pltpu.SMEM(send_slab.shape, jnp.int32),
            pltpu.SMEM(send_cross.shape, jnp.int32),
            pltpu.SemaphoreType.DMA((3,)),
        ],
        compiler_params=small,
    )(weights.reshape(depth, out_channels), grad, neighbours, send_slab, send_cross)

    near = NEAR if owners == 512 else tuple(range(owners.bit_length() // 2))
    far = tuple(bit for bit in range(owners.bit_length() - 1) if bit not in near)
    arrived = exchange(terms, near, owners)
    shared, slab_back = staged_sum(
        arrived, packed.shape[0] >> len(near) << len(far), 1 << len(far), [], backs[:2], small)
    arrived = exchange(shared, far, owners)
    slab_back = swap(*slab_back, "slab")
    shared, passed = staged_sum(
        arrived, packed.shape[0], 1 << len(near), slab_back, [partial, *backs[2:]], small)
    partial, cross_back = passed[0], swap(*passed[1:], "cross")
    gathered = exchange(shared, near, owners)
    scale = 1.0 / math.sqrt(owners * total)
    kernel_grad, bias_grad, grad_features = pl.pallas_call(
        lambda *refs: finish_kernel(scale, *refs),
        out_shape=[shape(weights.shape, f32), shape((1, out_channels), f32), shape(features.shape, bf16)],
        in_specs=[VMEM] * 7,
        out_specs=[VMEM] * 3,
        scratch_shapes=[pltpu.VMEM((TILE, voxels), bf16)],
        compiler_params=small,
    )(gathered, partial, flags, *slab_back, *cross_back)
    return grad_features, kernel_grad, bias_grad.reshape(out_channels)


def solution(mesh):
    in_specs = (
        P("slab", "cross", None, None, None),
        P("slab", "cross", None, None, None),
        P(),
        P(),
        P("slab", "cross"),
        P("slab", "cross", None, None),
        P("slab", "cross", None, None),
        P("slab", "cross", None, None),
    )
    out_specs = (P("slab", "cross", None, None, None), P(), P())
    return jax.shard_map(local, mesh=mesh, in_specs=in_specs, out_specs=out_specs, check_vma=False)
```

```python
import math

import jax
import jax.numpy as jnp
from jax import lax
from jax.experimental import pallas as pl
from jax.experimental.pallas import tpu as pltpu
from jax.sharding import PartitionSpec as P

EDGE = 8
LAYER = EDGE * EDGE
TILE = 2 * LAYER
PACK = 16
FIRST = 60 * 2**20
MIDDLE = 55_700_000
NEAR = (0, 1, 2, 3, 6)
f32 = jnp.float32
bf16 = jnp.bfloat16
VMEM = pl.BlockSpec(memory_space=pltpu.VMEM)
SMEM = pl.BlockSpec(memory_space=pltpu.SMEM)
HBM = pl.BlockSpec(memory_space=pltpu.HBM)
ANY = pl.BlockSpec(memory_space=pl.ANY)


def nn(a, b):
    return lax.dot_general(a, b, (((1,), (0,)), ((), ())), preferred_element_type=f32)


def nt(a, b):
    return lax.dot_general(a, b, (((1,), (1,)), ((), ())), preferred_element_type=f32)


def tn(a, b):
    return lax.dot_general(a, b, (((0,), (0,)), ((), ())), preferred_element_type=f32)


def layer_map(axis, voxels):
    row = lax.broadcasted_iota(jnp.int32, (TILE, voxels), 0)
    v = lax.broadcasted_iota(jnp.int32, (TILE, voxels), 1)
    x, y, z = v >> 6, (v >> 3) & 7, v & 7
    along, beside = (y, x * EDGE + z) if axis == 1 else (z, x * EDGE + y)
    low = (along == 0) & (row == beside)
    high = (along == EDGE - 1) & (row == beside + LAYER)
    return jnp.where(low | high, 1.0, 0.0).astype(bf16)


def low_half(rows):
    return lax.broadcasted_iota(jnp.int32, (rows, TILE), 1) < LAYER


def x_faces(brick):
    return jnp.where(low_half(brick.shape[0]), brick[:, :TILE], brick[:, -TILE:])


def doubled(tile):
    turned = pltpu.roll(tile, LAYER, 1)
    half = low_half(tile.shape[0])
    return jnp.where(half, tile, turned), jnp.where(half, turned, tile)


def fetch(sources, targets, arrivals):
    copies = [pltpu.make_async_copy(a, b, arrivals.at[k]) for k, (a, b) in enumerate(zip(sources, targets))]
    for copy in copies:
        copy.start()
    return copies


def choose(axis, even, odd):
    return jnp.where((lax.axis_index(axis) & 1) == 0, even, odd)


def to_peers(refs, up, down, cross_up, cross_down):
    for ref, tile in zip(refs, (choose("slab", down, up), choose("slab", up, down),
                                choose("cross", cross_down, cross_up), choose("cross", cross_up, cross_down))):
        ref[...] = tile.astype(bf16)


def from_peers(refs):
    far, near, cross_far, cross_near = [ref[...].astype(f32) for ref in refs]
    return (choose("slab", far, near), choose("slab", near, far),
            choose("cross", cross_far, cross_near), choose("cross", cross_near, cross_far))


def send_kernel(features_in, slab_in, cross_in, *refs):
    faces, (features, slab_list, cross_list, arrivals) = refs[:4], refs[4:]
    copies = fetch((features_in, slab_in, cross_in), (features, slab_list, cross_list), arrivals)
    number, channels, voxels = features.shape[2:]
    y_map = layer_map(1, voxels)
    for copy in copies:
        copy.wait()
    half = low_half(channels)
    tables = ([], [])
    for b in range(number):
        brick = features[0, 0, b]
        tables[0].append(doubled(x_faces(brick.astype(f32))))
        tables[1].append(doubled(nt(brick, y_map)))
    sends = []
    for axis, listed in enumerate((slab_list, cross_list)):
        for row in range(2):
            side = 1 - row
            picked = []
            for k in range(2):
                entry = listed[0, 0, row, k]
                value = jnp.zeros((channels, TILE), f32)
                for b in range(number):
                    value = jnp.where(entry == 6 * b + 2 * axis + side, tables[axis][b][side], value)
                picked.append(value)
            sends.append(jnp.where(half, picked[0], picked[1]))
    to_peers(faces, *sends)


def main_kernel(features_in, weights_in, upstream_in, bias_in, count_in, links_in, *refs):
    received, (terms, grad), refs = refs[:4], refs[4:6], refs[6:]
    features, weights, upstream, bias, count, links, fields, taps, table, marks, arrivals = refs
    copies = fetch(
        (features_in, links_in, weights_in, bias_in, count_in, upstream_in),
        (features, links, weights, bias, count, upstream), arrivals)
    number, channels, voxels = features.shape[2:]
    out_channels = upstream.shape[3]
    depth = 7 * channels
    total = number * voxels
    own = 6 * number
    half = low_half(channels)
    lane = lax.broadcasted_iota(jnp.int32, (channels, total), 1)
    v = lane & (voxels - 1)
    coords = (v >> 6, (v >> 3) & 7, v & 7)
    strides = (LAYER, EDGE, 1)
    for axis in (1, 2):
        marks[TILE * (axis - 1):TILE * axis] = layer_map(axis, voxels)
    copies[0].wait()

    cubes = jnp.concatenate([features[0, 0, b] for b in range(number)], axis=1)
    cubes32 = cubes.astype(f32)
    for b in range(number):
        brick = features[0, 0, b]
        table[6 * b], table[6 * b + 1] = doubled(x_faces(brick.astype(f32)))
        sides = nt(brick, marks[...])
        table[6 * b + 2], table[6 * b + 3] = doubled(sides[:, :TILE])
        table[6 * b + 4], table[6 * b + 5] = doubled(sides[:, TILE:])
    for k, tile in enumerate(from_peers(received)):
        table[own + 2 * k], table[own + 2 * k + 1] = doubled(tile)
    copies[1].wait()
    table[own + 8] = jnp.zeros((channels, TILE), f32)

    fields[:channels] = cubes
    for axis in range(3):
        expanded = []
        for b in range(number):
            tile = jnp.where(half, table[links[0, 0, b, 2 * axis]], table[links[0, 0, b, 2 * axis + 1]])
            if axis == 0:
                gap = jnp.zeros((channels, voxels - 2 * TILE), f32)
                expanded.append(jnp.concatenate([tile, gap, tile], axis=1))
            else:
                expanded.append(nn(tile.astype(bf16), marks[TILE * (axis - 1):TILE * axis]))
        outer = jnp.concatenate(expanded, axis=1)
        low = jnp.where(coords[axis] == 0, outer, pltpu.roll(cubes32, strides[axis], 1))
        high = jnp.where(coords[axis] == EDGE - 1, outer, pltpu.roll(cubes32, total - strides[axis], 1))
        fields[channels * (2 * axis + 1):channels * (2 * axis + 2)] = low.astype(bf16)
        fields[channels * (2 * axis + 2):channels * (2 * axis + 3)] = high.astype(bf16)
    fields[depth:] = jnp.ones((PACK, total), bf16)

    copies[2].wait()
    copies[3].wait()
    first = bias[...].astype(bf16)
    rest = bias[...] - first.astype(f32)
    second = rest.astype(bf16)
    third = (rest - second.astype(f32)).astype(bf16)
    row = lax.broadcasted_iota(jnp.int32, (PACK, out_channels), 0)
    extra = jnp.where(row == 0, first.astype(f32),
                      jnp.where(row == 1, second.astype(f32), jnp.where(row == 2, third.astype(f32), 0.0)))
    taps[:depth] = weights[...]
    taps[depth:] = extra.astype(bf16)

    pre = tn(taps[...], fields[...])
    copies[4].wait()
    copies[5].wait()
    grad[out_channels:] = jnp.zeros((grad.shape[0] - out_channels, total), bf16)
    for b in range(number):
        part = pre[:, voxels * b:voxels * (b + 1)]
        s = jax.nn.sigmoid(part)
        value = upstream[0, 0, b].astype(f32) * (s * (1.0 + part * (1.0 - s)))
        grad[:out_channels, voxels * b:voxels * (b + 1)] = jnp.where(b < count[0, 0], value, 0.0).astype(bf16)

    found = nt(fields[...], grad[...])
    middle = depth // 2
    terms[:depth] = found[:depth, :TILE].astype(bf16)
    terms[depth:depth + middle] = (found[:middle, TILE:] + pltpu.roll(found[middle:depth, TILE:], LAYER, 1)).astype(bf16)
    row = lax.broadcasted_iota(jnp.int32, (PACK, TILE), 0)
    terms[depth + middle:] = jnp.where(row == 0, found[depth:, :TILE],
                                       jnp.where(row == 1, found[depth:, TILE:], 0.0)).astype(bf16)


def list_places(number):
    return [(axis, side, b, place) for axis in range(2) for side in range(2) for b in range(number) for place in range(2)]


def back_kernel(weights, grad, links_in, slab_in, cross_in, *refs):
    sent, (partial, flags, marks, table_grad, links, slab_list, cross_list, arrivals) = refs[:4], refs[4:]
    copies = fetch((links_in, slab_in, cross_in), (links, slab_list, cross_list), arrivals)
    channels, total = partial.shape
    number = links.shape[2]
    voxels = total // number
    out_channels = weights.shape[1]
    own = 6 * number
    half = low_half(channels)
    v = lax.broadcasted_iota(jnp.int32, (channels, total), 1) & (voxels - 1)
    coords = (v >> 6, (v >> 3) & 7, v & 7)
    strides = (LAYER, EDGE, 1)
    for axis in (1, 2):
        marks[TILE * (axis - 1):TILE * axis] = layer_map(axis, voxels)
    table_grad[...] = jnp.zeros(table_grad.shape, f32)
    for copy in copies:
        copy.wait()
    row = lax.broadcasted_iota(jnp.int32, flags.shape, 0)
    named = jnp.zeros(flags.shape, f32)
    for k, (axis, side, b, place) in enumerate(list_places(number)):
        entry = (slab_list, cross_list)[axis][0, 0, 1 - side, place]
        named = jnp.where((row == k) & (entry == 6 * b + 2 * axis + side), 1.0, named)
    flags[...] = named
    live = grad[:out_channels]
    summed = nn(weights[:channels], live)
    for axis in range(3):
        low = nn(weights[channels * (2 * axis + 1):channels * (2 * axis + 2)], live)
        high = nn(weights[channels * (2 * axis + 2):channels * (2 * axis + 3)], live)
        at = coords[axis]
        summed = summed + jnp.where(at < EDGE - 1, pltpu.roll(low, total - strides[axis], 1), 0.0)
        summed = summed + jnp.where(at > 0, pltpu.roll(high, strides[axis], 1), 0.0)
        edge = jnp.where(at == 0, low, high)
        for b in range(number):
            brick = edge[:, voxels * b:voxels * (b + 1)]
            if axis == 0:
                tile = x_faces(brick)
            else:
                tile = nt(brick.astype(bf16), marks[TILE * (axis - 1):TILE * axis])
            to_low, to_high = doubled(tile)
            table_grad[links[0, 0, b, 2 * axis]] = to_low
            table_grad[links[0, 0, b, 2 * axis + 1]] = to_high
    low, high, cross_low, cross_high = [
        jnp.where(half, table_grad[own + 2 * k], table_grad[own + 2 * k + 1]) for k in range(4)]
    to_peers(sent, high, low, cross_high, cross_low)
    for b in range(number):
        parts = summed[:, voxels * b:voxels * (b + 1)]
        for axis in range(3):
            tile = jnp.where(half, table_grad[6 * b + 2 * axis], table_grad[6 * b + 2 * axis + 1])
            parts = parts + spread(tile, axis, marks, voxels)
        partial[:, voxels * b:voxels * (b + 1)] = parts


def spread(tile, axis, marks, voxels):
    if axis > 0:
        return nn(tile.astype(bf16), marks[TILE * (axis - 1):TILE * axis])
    half = low_half(tile.shape[0])
    gap = jnp.zeros((tile.shape[0], voxels - 2 * TILE), f32)
    return jnp.concatenate([jnp.where(half, tile, 0.0), gap, jnp.where(half, 0.0, tile)], axis=1)


def sum_chunks(arrived, shared, parts):
    rows = shared.shape[0] // parts
    value = jnp.sum(arrived[...].astype(f32).reshape(arrived.shape[0] // rows, rows, TILE), axis=0).astype(bf16)
    shared[...] = jnp.broadcast_to(value[None], (parts, rows, TILE)).reshape(shared.shape)


def finish_kernel(scale, gathered, partial, flags, slab_far, slab_near, cross_far, cross_near,
                  kernel_grad, bias_grad, result, marks):
    unpack(scale, gathered, kernel_grad, bias_grad)
    number, channels, voxels = result.shape[2:]
    half = low_half(channels)
    marks[...] = layer_map(1, voxels)
    second, first, cross_second, cross_first = from_peers((slab_far, slab_near, cross_far, cross_near))
    faces = [[doubled(back) for back in backs] for backs in ((second, first), (cross_second, cross_first))]
    sides = {}
    for k, (axis, side, b, place) in enumerate(list_places(number)):
        value = flags[k:k + 1] * faces[axis][side][place]
        sides[axis, side, b] = sides[axis, side, b] + value if place else value
    for b in range(number):
        parts = partial[:, voxels * b:voxels * (b + 1)]
        for axis in range(2):
            parts = parts + spread(jnp.where(half, sides[axis, 0, b], sides[axis, 1, b]), axis, marks, voxels)
        result[0, 0, b] = parts.astype(bf16)


def unpack(scale, gathered, kernel_grad, bias_grad):
    taps, channels, out_channels = kernel_grad.shape
    depth = taps * channels
    middle = depth // 2
    wide = gathered[...].astype(f32) * scale
    rest = wide[depth:depth + middle]
    second = jnp.concatenate([rest, pltpu.roll(rest, LAYER, 1)], axis=0)
    for tap in range(taps):
        rows = slice(channels * tap, channels * (tap + 1))
        kernel_grad[tap, :, :TILE] = wide[rows]
        kernel_grad[tap, :, TILE:] = second[rows, :out_channels - TILE]
    bias_grad[:, :TILE] = wide[depth + middle:depth + middle + 1]
    bias_grad[:, TILE:] = wide[depth + middle + 1:depth + middle + 2, :out_channels - TILE]


def groups_of(bits, count):
    mask = sum(1 << bit for bit in bits)
    found = {}
    for device in range(count):
        found.setdefault(device & ~mask, []).append(device)
    return list(found.values())


def swap(far, near, axis):
    def pairs(value, first):
        lows = range(first, lax.axis_size(axis) - 1, 2)
        return lax.ppermute(value, axis, [pair for low in lows for pair in ((low, low + 1), (low + 1, low))])

    return pairs(far, 1), pairs(near, 0)


def swap_one(value, axis, first):
    lows = range(first, lax.axis_size(axis) - 1, 2)
    return lax.ppermute(value, axis, [pair for low in lows for pair in ((low, low + 1), (low + 1, low))])


def staged_sum(arrived, rows, parts, ended, passed, params):
    shared, *passed = pl.pallas_call(
        lambda arrived, *refs: sum_chunks(arrived, refs[len(ended) + len(passed)], parts),
        out_shape=[shape((rows, TILE), bf16)] + [shape(x.shape, x.dtype) for x in passed],
        in_specs=[VMEM] + [ANY] * (len(ended) + len(passed)),
        out_specs=[VMEM] + [ANY] * len(passed),
        input_output_aliases={1 + len(ended) + k: 1 + k for k in range(len(passed))},
        compiler_params=params,
    )(arrived, *ended, *passed)
    return shared, passed


def exchange(value, bits, count):
    return lax.all_to_all(value, ("slab", "cross"), 0, 0, axis_index_groups=groups_of(bits, count), tiled=True)


def shape(dims, dtype):
    return jax.ShapeDtypeStruct(dims, dtype)


def local(features, out_grad, weights, conv_bias, brick_count, neighbours, send_slab, send_cross):
    number, channels, voxels = features.shape[2:]
    out_channels = out_grad.shape[3]
    depth = 7 * channels
    total = number * voxels
    owners = lax.axis_size("slab") * lax.axis_size("cross")
    face_pair = shape((channels, TILE), bf16)
    limit = pltpu.CompilerParams(vmem_limit_bytes=FIRST)
    middle = pltpu.CompilerParams(vmem_limit_bytes=MIDDLE)
    small = pltpu.CompilerParams(vmem_limit_bytes=16 * 2**20)

    sends = pl.pallas_call(
        send_kernel,
        out_shape=[face_pair] * 4,
        in_specs=[HBM] * 3,
        out_specs=[VMEM] * 4,
        scratch_shapes=[
            pltpu.VMEM(features.shape, bf16),
            pltpu.SMEM(send_slab.shape, jnp.int32),
            pltpu.SMEM(send_cross.shape, jnp.int32),
            pltpu.SemaphoreType.DMA((3,)),
        ],
        compiler_params=limit,
    )(features, send_slab, send_cross)
    packed = shape((depth * 3 // 2 + PACK, TILE), bf16)
    terms, grad = pl.pallas_call(
        main_kernel,
        out_shape=[packed, shape((2 * TILE, total), bf16)],
        in_specs=[HBM] * 6 + [VMEM] * 4,
        out_specs=[VMEM] * 2,
        scratch_shapes=[
            pltpu.VMEM(features.shape, bf16),
            pltpu.VMEM((depth, out_channels), bf16),
            pltpu.VMEM(out_grad.shape, bf16),
            pltpu.VMEM((1, out_channels), f32),
            pltpu.SMEM(brick_count.shape, jnp.int32),
            pltpu.SMEM(neighbours.shape, jnp.int32),
            pltpu.VMEM((depth + PACK, total), bf16),
            pltpu.VMEM((depth + PACK, out_channels), bf16),
            pltpu.VMEM((6 * number + 9, channels, TILE), f32),
            pltpu.VMEM((2 * TILE, voxels), bf16),
            pltpu.SemaphoreType.DMA((6,)),
        ],
        compiler_params=middle,
    )(features, weights.reshape(depth, out_channels), out_grad, conv_bias.reshape(1, out_channels), brick_count,
      neighbours, *swap(*sends[:2], "slab"), *swap(*sends[2:], "cross"))
    *backs, partial, flags = pl.pallas_call(
        back_kernel,
        out_shape=[face_pair] * 4 + [shape((channels, total), f32), shape((len(list_places(number)), TILE), f32)],
        in_specs=[VMEM, VMEM] + [HBM] * 3,
        out_specs=[VMEM] * 6,
        scratch_shapes=[
            pltpu.VMEM((2 * TILE, voxels), bf16),
            pltpu.VMEM((6 * number + 9, channels, TILE), f32),
            pltpu.SMEM(neighbours.shape, jnp.int32),
            pltpu.SMEM(send_slab.shape, jnp.int32),
            pltpu.SMEM(send_cross.shape, jnp.int32),
            pltpu.SemaphoreType.DMA((3,)),
        ],
        compiler_params=small,
    )(weights.reshape(depth, out_channels), grad, neighbours, send_slab, send_cross)

    near = NEAR if owners == 512 else tuple(range(owners.bit_length() // 2))
    far = tuple(bit for bit in range(owners.bit_length() - 1) if bit not in near)
    arrived = exchange(terms, near, owners)
    shared, (slab_far, cross_far) = staged_sum(
        arrived, packed.shape[0] >> len(near) << len(far), 1 << len(far), [], [backs[0], backs[2]], small)
    arrived = exchange(shared, far, owners)
    back_far = [swap_one(slab_far, "slab", 1), swap_one(cross_far, "cross", 1)]
    shared, (partial, slab_near, cross_near) = staged_sum(
        arrived, packed.shape[0], 1 << len(near), back_far, [partial, backs[1], backs[3]], small)
    slab_back = back_far[0], swap_one(slab_near, "slab", 0)
    cross_back = back_far[1], swap_one(cross_near, "cross", 0)
    gathered = exchange(shared, near, owners)
    scale = 1.0 / math.sqrt(owners * total)
    kernel_grad, bias_grad, grad_features = pl.pallas_call(
        lambda *refs: finish_kernel(scale, *refs),
        out_shape=[shape(weights.shape, f32), shape((1, out_channels), f32), shape(features.shape, bf16)],
        in_specs=[VMEM] * 7,
        out_specs=[VMEM] * 3,
        scratch_shapes=[pltpu.VMEM((TILE, voxels), bf16)],
        compiler_params=small,
    )(gathered, partial, flags, *slab_back, *cross_back)
    return grad_features, kernel_grad, bias_grad.reshape(out_channels)


def solution(mesh):
    in_specs = (
        P("slab", "cross", None, None, None),
        P("slab", "cross", None, None, None),
        P(),
        P(),
        P("slab", "cross"),
        P("slab", "cross", None, None),
        P("slab", "cross", None, None),
        P("slab", "cross", None, None),
    )
    out_specs = (P("slab", "cross", None, None, None), P(), P())
    return jax.shard_map(local, mesh=mesh, in_specs=in_specs, out_specs=out_specs, check_vma=False)
```
